512 devices in a mesh: gx: 16 (over y, core), gy: 32 (over z, x).
Axes of the slice: x: 4, y: 8, z: 8, core: 2. Of those that a mesh axis runs over, the one named last changes fastest.
Arguments:
- right_side: float32 [688, 928, 128], P('gx', 'gy'), may hold values from -6 to 6
- diffusion: float32 [96, 128, 18], P('gx', 'gy'), may hold values from 0.2 to 5
- inverse_correlation_squared: float32 [96, 128, 18], P('gx', 'gy'), may hold values from 0.5 to 8
- widths_x: int32 [16], P('gx'), may hold values from 1 to 6, 48 in all
- widths_y: int32 [32], P('gy'), may hold values from 1 to 4, 64 in all
- coarse_factor: float32 [8192, 8192], P(('gx', 'gy')), may hold values from -0.00390625 to 0.00390625
Outputs:
- solution_field: float32 [688, 928, 128], P('gx', 'gy')
- residual: float32 [688, 928, 128], P('gx', 'gy')
The draws below stay inside these ranges and needn't reach their ends.
Inputs may be any that keep to these rules, and one draw needn't show every extreme that they name: `widths_x`: each entry is the element columns of one partition along the first direction; they sum to 3 times the number of partitions along gx, and some partition has exactly 6. `widths_y`: each entry is the element columns of one partition along the second direction; they sum to 2 times the number of partitions along gy, and some partition has exactly 4.
All inputs are finite; a program needn't handle non-finite values. No bound on the sum of `widths_x` or of `widths_y` on one device may be relied on, other than what follows from the above.
Results may differ from the reference program's by a relative error of at most 0.029.
Values sent between devices are 32-bit elements; how exact they have to be, the bound alone decides.
A program may use at most 64 MiB of HBM per device.

```python
import math
import jax
import jax.numpy as jnp
import numpy as np
from jax import lax

EX = 3
EY = 2
VERTICAL_CELLS = 18
ZP = 128
ZC = 16
ITERS = 3
MOST_COLUMNS_X = 6
MOST_COLUMNS_Y = 4
SX = 43
SY = 29
NC = 8192
N_GX = 16
N_GY = 32


def steps_of(rng, extent, pieces, low, top_value):
    factor_of, own = 1.0, jax.random.fold_in(rng, 6)
    for dim, blocks in pieces:
        draws = jnp.exp(jax.random.uniform(jax.random.fold_in(own, dim), (blocks,), jnp.float32, low / len(pieces), top_value / len(pieces)))
        factor_of = factor_of * jnp.repeat(draws, extent[dim] // blocks).reshape([-1 if axis == dim else 1 for axis in range(len(extent))])
    return factor_of


def length_profile(amount, total, reach, skew):
    portions = [(1 << 20) // math.isqrt(standing ** skew) + 1 for standing in range(2, amount + 1)]
    spare, given = total - reach - (amount - 1), [1] * (amount - 1)
    while spare > 0:
        candidates = [i for i in range(amount - 1) if given[i] < reach]
        whole, remaining = sum([portions[i] for i in candidates]), spare
        for i in candidates:
            more = min(reach - given[i], max(1, remaining * portions[i] // whole), spare)
            given[i] = given[i] + more
            spare = spare - more
    return np.array([reach] + given)


def ragged(own_key, count, total, bound, slope):
    if count == 2:
        one = jax.random.randint(own_key, (), max(1, total - bound), min(bound, total - 1) + 1)
        return jnp.stack([one, total - one])
    sizes = jnp.asarray(length_profile(count, total, bound, slope), jnp.int32)
    twos = (count - 1) // 2
    donor, sink = sizes[1:1 + 2 * twos:2], sizes[2:2 + 2 * twos:2]
    room = jnp.minimum(donor - 1, bound - sink)
    passed = jax.random.randint(jax.random.fold_in(own_key, 1), (twos,), 0, 1 << 20) % (room + 1)
    sizes = sizes.at[1:1 + 2 * twos:2].set(donor - passed).at[2:2 + 2 * twos:2].set(sink + passed)
    return sizes[jax.random.permutation(jax.random.fold_in(own_key, 2), count)]


def noise(own_key, dims, scale, bound, cuts=(), held_as=jnp.bfloat16):
    values = jax.random.normal(own_key, dims, jnp.float32) * scale
    if len(cuts) > 0:
        values = steps_of(own_key, dims, cuts, -0.22, 0.18) * values
    return jnp.clip(values, min=-bound, max=bound).astype(held_as)


def setup_inputs(seed: int = 0) -> dict:
    keys = jax.random.split(jax.random.key(seed), 7)
    right_side = noise(keys[0], (N_GX * SX, N_GY * SY, ZP), 1.0, 6.0, ((0, 16), (1, 32)), jnp.float32)
    diffusion = jnp.clip(jnp.exp(math.log(5.0) - 3.218876 * jax.random.uniform(keys[1], (N_GX * MOST_COLUMNS_X, N_GY * MOST_COLUMNS_Y, VERTICAL_CELLS), jnp.float32) ** steps_of(keys[1], (N_GX * MOST_COLUMNS_X, N_GY * MOST_COLUMNS_Y, VERTICAL_CELLS), ((0, 16), (1, 32)), -0.2, 0.2)), 0.2, 5.0)
    inverse_correlation_squared = jnp.clip(jnp.exp(math.log(8.0) - 2.7725887 * jax.random.uniform(keys[2], (N_GX * MOST_COLUMNS_X, N_GY * MOST_COLUMNS_Y, VERTICAL_CELLS), jnp.float32) ** steps_of(keys[2], (N_GX * MOST_COLUMNS_X, N_GY * MOST_COLUMNS_Y, VERTICAL_CELLS), ((0, 16), (1, 32)), -0.2, 0.2)), 0.5, 8.0)
    widths_x = ragged(keys[3], N_GX, EX * N_GX, MOST_COLUMNS_X, 2).astype(jnp.int32)
    widths_y = ragged(keys[4], N_GY, EY * N_GY, MOST_COLUMNS_Y, 2).astype(jnp.int32)
    coarse_factor = noise(keys[5], (NC, NC), (300 * NC) ** -0.5, 0.00390625, ((0, 512),), jnp.float32)
    return {"right_side": right_side, "diffusion": diffusion, "inverse_correlation_squared": inverse_correlation_squared, "widths_x": widths_x, "widths_y": widths_y, "coarse_factor": coarse_factor}


HIGHEST = lax.Precision.HIGHEST


def gll_weights():
    return np.array([1.0 / 28.0, 0.2107042271435061, 0.3411226924835044, 0.4124587946587038,
                     0.4124587946587038, 0.3411226924835044, 0.2107042271435061, 1.0 / 28.0])


def gll_derivative():
    points = np.array([-1.0, -0.8717401485096066, -0.5917001814331423, -0.2092992179024789,
                       0.2092992179024789, 0.5917001814331423, 0.8717401485096066, 1.0])
    identity = np.eye(8) > 0
    spacing = np.where(identity, 1.0, points[:, None] - points[None, :])
    barycentric = 1.0 / np.prod(spacing, axis=1)
    matrix = np.where(identity, 0.0, (barycentric[None, :] / barycentric[:, None]) / spacing)
    return np.where(identity, -np.sum(matrix, axis=1)[:, None], matrix)


def local_index(count):
    return (7 * jnp.arange(count, dtype=jnp.int32)[:, None] + jnp.arange(8, dtype=jnp.int32)[None, :]).reshape(-1)


def spread(values, axis):
    weights = jnp.asarray(gll_weights(), jnp.float32)
    moved = jnp.moveaxis(values, axis, 0)
    count = moved.shape[0]
    shaped = weights.reshape((1, 8) + (1,) * (moved.ndim - 1))
    expanded = (moved[:, None] * shaped).reshape((8 * count,) + moved.shape[1:])
    return jnp.moveaxis(expanded, 0, axis)


def to_nodes(values, axis):
    moved = jnp.moveaxis(values, axis, 0)
    count = moved.shape[0] // 8
    summed = jax.ops.segment_sum(moved, local_index(count), num_segments=7 * count + 1)
    return jnp.moveaxis(summed, 0, axis)


def to_points(values, axis):
    count = (values.shape[axis] - 1) // 7
    return jnp.take(values, local_index(count), axis=axis)


def local_derivative(points, axis, matrix):
    moved = jnp.moveaxis(points, axis, 0)
    count = moved.shape[0] // 8
    blocks = moved.reshape((count, 8) + moved.shape[1:])
    result = jnp.einsum('ab,nb...->na...', matrix, blocks, precision=HIGHEST)
    return jnp.moveaxis(result.reshape(moved.shape), 0, axis)


def storage_nodes(width, capacity):
    slots = jnp.arange(7 * capacity + 1, dtype=jnp.int32)
    return jnp.where(slots < 7 * width, slots, jnp.where(slots == 7 * capacity, 7 * width, -1))


def global_ids(widths, capacity):
    offsets = jnp.cumsum(widths) - widths
    local = jax.vmap(lambda width: storage_nodes(width, capacity))(widths)
    return jnp.where(local >= 0, local + 7 * offsets[:, None], -1).reshape(-1)


def element_index_list(widths, capacity):
    offsets = jnp.cumsum(widths) - widths
    slots = jnp.arange(capacity, dtype=jnp.int32)
    return jnp.where(slots[None, :] < widths[:, None], slots[None, :] + offsets[:, None], -1).reshape(-1)


def collect(values, ids, count, axis):
    moved = jnp.moveaxis(values, axis, 0)
    target = jnp.where(ids < 0, count, ids).astype(jnp.int32)
    summed = jax.ops.segment_sum(moved, target, num_segments=count + 1)[:count]
    return jnp.moveaxis(summed, 0, axis)


def distribute(values, ids, axis):
    moved = jnp.moveaxis(values, axis, 0)
    taken = jnp.take(moved, jnp.maximum(ids, 0).astype(jnp.int32), axis=0)
    usable = (ids >= 0).reshape((-1,) + (1,) * (moved.ndim - 1))
    return jnp.moveaxis(jnp.where(usable, taken, 0.0), 0, axis)


def share_matrix(widths, count):
    offsets = jnp.cumsum(widths) - widths
    node = jnp.arange(count, dtype=jnp.int32)
    inside = (node[None, :] >= 7 * offsets[:, None]) & (node[None, :] <= 7 * (offsets + widths)[:, None])
    shared_nodes = jnp.any(node[None, :] == 7 * offsets[1:, None], axis=0)
    return jnp.where(inside, jnp.where(shared_nodes, 0.5, 1.0)[None, :], 0.0).astype(jnp.float32)


def coarse_gather(values, first, second, vertical):
    section = jnp.einsum('pn,nmk->pmk', first, values, precision=HIGHEST)
    section = jnp.einsum('qm,pmk->pqk', second, section, precision=HIGHEST)
    section = jnp.einsum('ck,pqk->pqc', vertical, section, precision=HIGHEST)
    return section.reshape(-1)


def coarse_spread(values, first, second, vertical):
    section = values.reshape(first.shape[0], second.shape[0], vertical.shape[0])
    section = jnp.einsum('ck,pqc->pqk', vertical, section, precision=HIGHEST)
    section = jnp.einsum('qm,pqk->pmk', second, section, precision=HIGHEST)
    return jnp.einsum('pn,pmk->nmk', first, section, precision=HIGHEST)


def reference(right_side, diffusion, inverse_correlation_squared, widths_x, widths_y, coarse_factor):
    vertical_node_count = 7 * VERTICAL_CELLS + 1
    count_first = 7 * EX * N_GX + 1
    count_second = 7 * EY * N_GY + 1
    ids_first = global_ids(widths_x, 2 * EX)
    ids_second = global_ids(widths_y, 2 * EY)
    elements_first = element_index_list(widths_x, 2 * EX)
    elements_second = element_index_list(widths_y, 2 * EY)
    diffuse = collect(collect(diffusion, elements_first, EX * N_GX, 0), elements_second, EY * N_GY, 1)
    kappa = collect(collect(inverse_correlation_squared, elements_first, EX * N_GX, 0), elements_second, EY * N_GY, 1)
    load = collect(collect(right_side[:, :, :vertical_node_count], ids_first, count_first, 0), ids_second, count_second, 1)

    coef_first = spread(to_nodes(spread(to_nodes(spread(diffuse, 1), 1), 2), 2), 0)
    coef_second = spread(to_nodes(spread(to_nodes(spread(diffuse, 0), 0), 2), 2), 1)
    coef_vertical = spread(to_nodes(spread(to_nodes(spread(diffuse, 0), 0), 1), 1), 2)
    mass = to_nodes(spread(to_nodes(spread(to_nodes(spread(kappa, 0), 0), 1), 1), 2), 2)
    derivative = jnp.asarray(gll_derivative(), jnp.float32)
    coefficients = ((0, coef_first), (1, coef_second), (2, coef_vertical))

    def operate(field):
        total = mass * field
        for axis, coefficient in coefficients:
            gradient = local_derivative(to_points(field, axis), axis, derivative)
            total = total + to_nodes(local_derivative(coefficient * gradient, axis, derivative.T), axis)
        return total

    diagonal = mass
    for axis, coefficient in coefficients:
        diagonal = diagonal + to_nodes(local_derivative(coefficient, axis, (derivative * derivative).T), axis)

    share_first = share_matrix(widths_x, count_first)
    share_second = share_matrix(widths_y, count_second)
    block = ZP // ZC
    share_vertical = (jnp.arange(vertical_node_count, dtype=jnp.int32)[None, :] // block
                      == jnp.arange(ZC, dtype=jnp.int32)[:, None]).astype(jnp.float32)

    def precondition(resid):
        coarse_rhs = coarse_gather(resid, share_first, share_second, share_vertical)
        through = jnp.dot(coarse_rhs, coarse_factor, precision=HIGHEST)
        coarse_values = jnp.dot(coarse_factor, through, precision=HIGHEST)
        return resid / diagonal + coarse_spread(coarse_values, share_first, share_second, share_vertical)

    solution = jnp.zeros_like(load)
    resid = load
    smoothed = precondition(resid)
    direction = smoothed
    rho_now = jnp.sum(resid * smoothed)
    for iteration in range(ITERS):
        image = operate(direction)
        step_size = rho_now / jnp.sum(direction * image)
        solution = solution + step_size * direction
        resid = resid - step_size * image
        if iteration + 1 < ITERS:
            smoothed = precondition(resid)
            rho_next = jnp.sum(resid * smoothed)
            direction = smoothed + (rho_next / rho_now) * direction
            rho_now = rho_next

    def to_storage(values):
        placed = distribute(distribute(values, ids_first, 0), ids_second, 1)
        return jnp.pad(placed, ((0, 0), (0, 0), (0, ZP - vertical_node_count)))

    return to_storage(solution), to_storage(resid)
```

```python
import functools

import jax
import jax.numpy as jnp
import ml_dtypes
import numpy as np
from jax import lax
from jax.experimental import pallas as pl
from jax.experimental.pallas import tpu as pltpu
from jax.sharding import PartitionSpec as P

ITERS = 3
HIGHEST = lax.Precision.HIGHEST
MESH = pl.DeviceIdType.MESH
LANES = 128
ROWS = 32
PLANES = 48
DIRECTIONS = [(1, 0), (-1, 0), (0, 1), (0, -1), (1, 1), (1, -1), (-1, 1), (-1, -1)]


def gll_weights():
    return np.array(
        [
            1.0 / 28.0,
            0.2107042271435061,
            0.3411226924835044,
            0.4124587946587038,
            0.4124587946587038,
            0.3411226924835044,
            0.2107042271435061,
            1.0 / 28.0,
        ]
    )


def gll_derivative():
    points = np.array(
        [
            -1.0,
            -0.8717401485096066,
            -0.5917001814331423,
            -0.2092992179024789,
            0.2092992179024789,
            0.5917001814331423,
            0.8717401485096066,
            1.0,
        ]
    )
    identity = np.eye(8) > 0
    spacing = np.where(identity, 1.0, points[:, None] - points[None, :])
    barycentric = 1.0 / np.prod(spacing, axis=1)
    matrix = np.where(identity, 0.0, barycentric[None, :] / barycentric[:, None] / spacing)
    return np.where(identity, -np.sum(matrix, axis=1)[:, None], matrix)


WEIGHTS = gll_weights()
STIFF = gll_derivative().T @ np.diag(WEIGHTS) @ gll_derivative()


def split(matrix):
    high = matrix.astype(ml_dtypes.bfloat16)
    low = (matrix - high.astype(np.float64)).astype(ml_dtypes.bfloat16)
    return high, low


def band(cells, size):
    first, second = np.zeros((size, size)), np.zeros((size, size))
    for e in range(cells):
        for b in range(7):
            first[7 * e + b, 7 * e : 7 * e + 8] = STIFF[b]
        second[7 * e + 7, 7 * e : 7 * e + 8] = STIFF[7]
    return first, second


def tables(cap_x, cap_y, layers):
    first, second = band(layers, LANES)
    high, low = split(np.concatenate([first, second], axis=0).T)
    vertical = np.concatenate([high, high, low], axis=0)
    first, second = band(cap_y, ROWS)
    stacked = np.concatenate([np.kron(np.eye(4), first), np.kron(np.eye(4), second)], axis=0)
    high, low = split(stacked)
    across = np.concatenate([high, high, low], axis=1)
    depth = np.zeros((LANES, 3 * LANES))
    for h in range(layers):
        depth[h, 7 * h : 7 * h + 8] = WEIGHTS
        depth[h, LANES + 7 * h : LANES + 7 * h + 7] = 1.0
        depth[h, 2 * LANES + 7 * h + 7] = 1.0
    weigh, pick, ends = np.zeros((ROWS, 8)), np.zeros((ROWS, 8)), np.zeros((ROWS, 8))
    for f in range(cap_y):
        weigh[7 * f : 7 * f + 8, f] = WEIGHTS
        pick[7 * f : 7 * f + 7, f] = 1.0
        ends[7 * f + 7, f] = 1.0
    unit = np.eye(cap_x)
    widen = np.concatenate([np.kron(unit, weigh), np.kron(unit, pick), np.kron(unit, ends)], axis=0)
    widen = np.pad(widen, ((0, 0), (0, LANES - widen.shape[1])))
    factor = np.zeros((ROWS + 8, LANES))
    factor[: 7 * cap_y] = STIFF[np.arange(7 * cap_y) % 7, np.arange(7 * cap_y) % 7][:, None]
    factor[ROWS:, : 7 * layers] = STIFF[np.arange(7 * layers) % 7, np.arange(7 * layers) % 7][None, :]
    return (
        vertical,
        across,
        depth.astype(np.float32),
        widen.astype(np.float32),
        factor.astype(np.float32),
    )


def plane(x):
    return pl.ds(pl.multiple_of(x * ROWS, ROWS), ROWS)


def total(values):
    return jnp.sum(values, axis=(0, 1), keepdims=True)


def iota(shape, dim):
    return lax.broadcasted_iota(jnp.int32, shape, dim)


def kernel(
    nx, ny, cap_x, cap_y, layers,
    wx_ref, wy_ref, load_ref, diff_ref, kappa_ref, factor_ref,
    vertical_ref, across_ref, depth_ref, widen_ref, coefficient_ref,
    solution_ref, residual_ref,
    f_d, f_im, f_r, f_sol, f_inv, f_wid, f_mass, f_ya, f_yb, f_za, f_zb,
    e_px, e_big, e_ya, e_yb, squares, sq_kappa, t_now,
    halo_sx, halo_sy, halo_sc, halo_rx, halo_ry, halo_rc,
    coarse_s, coarse_r, part, recv1, msg2, recv2, msg3, recv3,
    last_s, last_r, last_s3, last_r3,
    h_send, h_recv, c_send, c_recv, r_send, r_recv, l_send, l_recv,
):
    p, q = lax.axis_index("gx"), lax.axis_index("gy")
    wx, wy = wx_ref[0], wy_ref[0]
    groups = part.shape[2]
    end_x, end_y = 7 * wx, 7 * wy

    def beside(dx, dy):
        return (lax.rem(p + dx + nx, nx), lax.rem(q + dy + ny, ny))

    barrier = pltpu.get_barrier_semaphore()

    def greet_gx(o, _):
        pl.semaphore_signal(barrier, inc=1, device_id=beside(o, 0), device_id_type=MESH)
        return 0

    def greet_gy(o, _):
        pl.semaphore_signal(barrier, inc=1, device_id=beside(0, o), device_id_type=MESH)
        return 0

    lax.fori_loop(1, nx, greet_gx, 0)
    lax.fori_loop(1, ny, greet_gy, 0)
    for dx, dy in DIRECTIONS[4:]:
        pl.semaphore_signal(barrier, inc=1, device_id=beside(dx, dy), device_id_type=MESH)

    def flag(condition):
        return jnp.where(condition, 1.0, 0.0).astype(jnp.float32)

    has_left, has_right = flag(p > 0), flag(p < nx - 1)
    has_below, has_above = flag(q > 0), flag(q < ny - 1)

    squares[...] = jnp.zeros_like(squares)
    sq_kappa[...] = jnp.zeros_like(sq_kappa)
    inside = iota((cap_y, layers), 0) < wy
    for e in range(cap_x):
        keep = inside & (e < wx)
        squares[8 * e : 8 * e + cap_y, 0:layers] = jnp.where(keep, diff_ref[e], 0.0)
        sq_kappa[8 * e : 8 * e + cap_y, 0:layers] = jnp.where(keep, kappa_ref[e], 0.0)
    deep = jnp.dot(squares[...], depth_ref[...], precision=HIGHEST, preferred_element_type=jnp.float32)
    deep_kappa = jnp.dot(
        sq_kappa[...], depth_ref[:, 0:LANES], precision=HIGHEST, preferred_element_type=jnp.float32
    )
    tall = cap_x * ROWS
    big = jnp.dot(
        widen_ref[0:tall, :],
        jnp.concatenate([deep, deep_kappa], axis=1),
        precision=HIGHEST,
        preferred_element_type=jnp.float32,
    )
    both = jnp.dot(
        widen_ref[tall : 3 * tall, :],
        deep[:, 0:LANES],
        precision=HIGHEST,
        preferred_element_type=jnp.float32,
    )
    zero_plane = jnp.zeros((ROWS, LANES), jnp.float32)
    for ref in (e_px, e_ya, e_yb):
        ref[0:ROWS, :] = zero_plane
        ref[tall + ROWS : tall + 2 * ROWS, :] = zero_plane
    for place in (0, tall + ROWS):
        e_big[place : place + ROWS, :] = jnp.zeros((ROWS, 3 * LANES), jnp.float32)
    e_px[ROWS : ROWS + tall, :] = big[:, 0:LANES]
    e_big[ROWS : ROWS + tall, :] = big[:, LANES : 4 * LANES]
    e_ya[ROWS : ROWS + tall, :] = both[0:tall]
    e_yb[ROWS : ROWS + tall, :] = both[tall : 2 * tall]

    for ref in (f_d, f_im, f_r, f_inv, f_wid, f_mass, f_ya, f_yb, f_za, f_zb):
        for x in range(7 * cap_x, PLANES):
            ref[x * ROWS : (x + 1) * ROWS, :] = zero_plane

    sources = (
        (f_za, e_big, 0), (f_zb, e_big, 1), (f_mass, e_big, 2), (f_ya, e_ya, 0), (f_yb, e_yb, 0),
    )
    row_factor = coefficient_ref[0:ROWS, :]
    depth_factor = coefficient_ref[ROWS : ROWS + 1, :]
    corner = float(STIFF[7, 7])

    def fill_plane(x, e, b):
        values = []
        for target, source, lane in sources:
            lanes = slice(lane * LANES, (lane + 1) * LANES)
            value = float(WEIGHTS[b]) * source[plane(e + 1), lanes]
            if b == 0:
                value = value + float(WEIGHTS[7]) * source[plane(e), lanes]
            target[plane(x), :] = value
            values.append(value)
        za, zb, mass, ya, yb = values
        diagonal = mass + ya * row_factor + yb * corner + za * depth_factor + zb * corner
        diagonal = diagonal + float(STIFF[b, b]) * e_px[plane(e + 1), :]
        if b == 0:
            diagonal = diagonal + float(STIFF[7, 7]) * e_px[plane(e), :]
        f_inv[plane(x), :] = diagonal

    def fill(e, _):
        for b in range(7):
            fill_plane(7 * e + b, e, b)
        return 0

    lax.fori_loop(0, cap_x, fill, 0)
    fill_plane(7 * cap_x, cap_x, 0)

    slots_x, slots_y = load_ref.shape[0], load_ref.shape[1]
    row = iota((slots_y, LANES), 0)
    real = iota((slots_y, LANES), 1) <= 7 * layers
    f_r[...] = jnp.zeros_like(f_r)

    def take(x, _):
        value = jnp.where(x < end_x, load_ref[x], jnp.where(x == end_x, load_ref[slots_x - 1], 0.0))
        last = value[slots_y - 1 : slots_y, :]
        value = jnp.where(row < end_y, value, jnp.where(row == end_y, last, 0.0))
        f_r[pl.ds(pl.multiple_of(x * ROWS, ROWS), slots_y), :] = jnp.where(real, value, 0.0)
        return 0

    lax.fori_loop(0, slots_x, take, 0)

    def high_plane(ref):
        value = jnp.zeros((ROWS, LANES), jnp.float32)
        for j in range(1, cap_x + 1):
            value = value + jnp.where(wx == j, ref[7 * j * ROWS : (7 * j + 1) * ROWS, :], 0.0)
        return value

    def side(j):
        return pl.ds(7 * j, PLANES, stride=ROWS)

    def high_row(plane_value):
        value = jnp.zeros((1, LANES), jnp.float32)
        for j in range(1, cap_y + 1):
            value = value + jnp.where(wy == j, plane_value[7 * j : 7 * j + 1, :], 0.0)
        return value

    def remote(source, target, send, recv, device):
        return pltpu.make_async_remote_copy(
            src_ref=source,
            dst_ref=target,
            send_sem=send,
            recv_sem=recv,
            device_id=device,
            device_id_type=MESH,
        )

    def halo_copies(h):
        copies = []
        for k, (dx, dy) in enumerate(DIRECTIONS):
            if dy == 0:
                slot = (h, 0 if dx > 0 else 1)
                source, target = halo_sx.at[slot], halo_rx.at[slot]
            elif dx == 0:
                slot = (h, 0 if dy > 0 else 1)
                source, target = halo_sy.at[slot], halo_ry.at[slot]
            else:
                source, target = halo_sc.at[h, k - 4], halo_rc.at[h, k - 4]
            copies.append(remote(source, target, h_send.at[h, k], h_recv.at[h, k], beside(dx, dy)))
        return copies

    def halo_start(h, ref):
        low, high = ref[0:ROWS, :], high_plane(ref)
        halo_sx[h, 0] = high
        halo_sx[h, 1] = low
        above = jnp.zeros((PLANES, LANES), jnp.float32)
        for j in range(1, cap_y + 1):
            above = above + jnp.where(wy == j, ref[side(j), :], 0.0)
        halo_sy[h, 0] = above
        halo_sy[h, 1] = ref[side(0), :]
        rows = (high_row(high), high[0:1, :], high_row(low), low[0:1, :])
        for k, value in enumerate(rows):
            halo_sc[h, k] = jnp.broadcast_to(value, (8, LANES))
        copies = halo_copies(h)
        for copy in copies:
            copy.start()
        return copies

    place = iota((PLANES, LANES), 0)

    def halo_finish(h, ref, copies):
        for copy in copies:
            copy.wait()
        ref[0:ROWS, :] = ref[0:ROWS, :] + has_left * halo_rx[h, 0]
        from_right = has_right * halo_rx[h, 1]
        for j in range(1, cap_x + 1):
            rows = slice(7 * j * ROWS, (7 * j + 1) * ROWS)
            ref[rows, :] = ref[rows, :] + jnp.where(wx == j, from_right, 0.0)

        def line(side_value, near, far):
            side_value = side_value + jnp.where(place == 0, has_left * near[0:1, :], 0.0)
            return side_value + jnp.where(place == end_x, has_right * far[0:1, :], 0.0)

        below = has_below * line(halo_ry[h, 0], halo_rc[h, 0], halo_rc[h, 2])
        above = has_above * line(halo_ry[h, 1], halo_rc[h, 1], halo_rc[h, 3])
        ref[side(0), :] = ref[side(0), :] + below
        for j in range(1, cap_y + 1):
            ref[side(j), :] = ref[side(j), :] + jnp.where(wy == j, above, 0.0)

    pl.semaphore_wait(barrier, nx + ny + 2)
    load_copies = halo_start(0, f_r)
    diagonal_copies = halo_start(1, f_inv)
    halo_finish(0, f_r, load_copies)

    row32 = iota((ROWS, LANES), 0)
    share_low = jnp.where(row32 == 0, 1.0 - 0.5 * has_below, 1.0)
    share_row = jnp.where(row32 == end_y, 1.0 - 0.5 * has_above, share_low)
    block = LANES // 16

    def share_x(x):
        low = jnp.where(x == 0, 1.0 - 0.5 * has_left, 1.0)
        return jnp.where(x == end_x, 1.0 - 0.5 * has_right, low)

    chunk = 4 * ROWS
    chunks = (7 * cap_x + 4) // 4

    def coarse_sums(ref):
        def add(i, value):
            return value + jnp.sum(
                ref[pl.ds(pl.multiple_of(i * chunk, chunk), chunk), :].reshape(4, ROWS, LANES), axis=0
            )

        value = lax.fori_loop(0, chunks, add, jnp.zeros((ROWS, LANES), jnp.float32))
        value = value - 0.5 * has_left * ref[0:ROWS, :] - 0.5 * has_right * high_plane(ref)
        return jnp.sum(share_row * value, axis=0, keepdims=True)

    def reduce_start(a, ref):
        profile = coarse_sums(ref)
        mask = iota((16, LANES), 1) // block == iota((16, LANES), 0)
        column = jnp.sum(jnp.where(mask, profile, 0.0), axis=1, keepdims=True)
        for i in range(nx):
            for g in range(groups):
                lanes = slice((i * groups + g) * LANES, (i * groups + g + 1) * LANES)
                part[a, i, g : g + 1, :] = jnp.sum(factor_ref[:, lanes] * column, axis=0, keepdims=True)

        def send(o, _):
            peer = lax.rem(p + o, nx)
            remote(
                part.at[a, peer], recv1.at[a, p], r_send.at[a, 0], r_recv.at[a, 0], (peer, q)
            ).start()
            return 0

        lax.fori_loop(1, nx, send, 0)
        recv1[a, p] = part[a, p]

    def wait_in(buffer, count, send, recv, device):
        remote(buffer.at[pl.ds(0, count)], buffer.at[pl.ds(0, count)], send, recv, device).wait_recv()

    def wait_out(buffer, count, send, recv, device):
        remote(buffer.at[pl.ds(0, count)], buffer.at[pl.ds(0, count)], send, recv, device).wait_send()

    lane = iota((1, LANES), 1)

    def scalar_row(values):
        result = jnp.zeros((1, LANES), jnp.float32)
        for i, value in enumerate(values):
            result = jnp.where(lane == i, value, result)
        return result

    def pick(values, i):
        return total(jnp.where(lane == i, values, 0.0))

    def reduce_finish(a, scalars):
        wait_in(recv1.at[a], nx - 1, r_send.at[a, 0], r_recv.at[a, 0], beside(1, 0))
        msg2[a, 0:groups, :] = jnp.sum(recv1[a], axis=0)
        msg2[a, groups : groups + 1, :] = scalar_row(scalars)

        def send2(o, _):
            peer = lax.rem(q + o, ny)
            remote(
                msg2.at[a], recv2.at[a, q], r_send.at[a, 1], r_recv.at[a, 1], (p, peer)
            ).start()
            return 0

        lax.fori_loop(1, ny, send2, 0)
        recv2[a, q] = msg2[a]
        wait_in(recv2.at[a], ny - 1, r_send.at[a, 1], r_recv.at[a, 1], beside(0, 1))
        msg3[a] = jnp.sum(recv2[a], axis=0)

        def send3(o, _):
            peer = lax.rem(p + o, nx)
            remote(
                msg3.at[a], recv3.at[a, p], r_send.at[a, 2], r_recv.at[a, 2], (peer, q)
            ).start()
            return 0

        lax.fori_loop(1, nx, send3, 0)
        recv3[a, p] = msg3[a]
        wait_in(recv3.at[a], nx - 1, r_send.at[a, 2], r_recv.at[a, 2], beside(1, 0))
        sums = jnp.sum(recv3[a, :, groups : groups + 1, :], axis=0)
        wait_out(recv1.at[a], nx - 1, r_send.at[a, 0], r_recv.at[a, 0], beside(1, 0))
        wait_out(recv2.at[a], ny - 1, r_send.at[a, 1], r_recv.at[a, 1], beside(0, 1))
        wait_out(recv3.at[a], nx - 1, r_send.at[a, 2], r_recv.at[a, 2], beside(1, 0))
        return sums

    def coarse_start(a):
        value = jnp.zeros((16, LANES), jnp.float32)
        for i in range(nx):
            for g in range(groups):
                lanes = slice((i * groups + g) * LANES, (i * groups + g + 1) * LANES)
                value = value + factor_ref[:, lanes] * t_now[i, g : g + 1, :]
        column = jnp.sum(value, axis=1, keepdims=True)
        mask = iota((16, LANES), 1) // block == iota((16, LANES), 0)
        values = jnp.sum(jnp.where(mask, column, 0.0), axis=0, keepdims=True)
        coarse_s[a] = jnp.broadcast_to(values, (8, LANES))
        copies = []
        for k, (dx, dy) in enumerate(DIRECTIONS):
            copy = remote(
                coarse_s.at[a], coarse_r.at[a, k], c_send.at[a, k], c_recv.at[a, k], beside(dx, dy)
            )
            copy.start()
            copies.append(copy)
        return copies

    def next_direction(a, copies, beta):
        for copy in copies:
            copy.wait()
        own = coarse_s[a, 0:1, :]
        got = {step: coarse_r[a, k, 0:1, :] for k, step in enumerate(DIRECTIONS)}
        got[(0, 0)] = own

        def spread(dx):
            centre, low, high = got[(dx, 0)], got[(dx, 1)], got[(dx, -1)]
            value = jnp.where(row32 == 0, centre + 0.5 * has_below * (low - centre), centre)
            return jnp.where(row32 == end_y, value + 0.5 * has_above * (high - centre), value)

        middle = spread(0)
        near = middle + 0.5 * has_left * (spread(1) - middle)
        far = middle + 0.5 * has_right * (spread(-1) - middle)

        def update(x, _):
            inv = f_inv[plane(x), :]
            coarse = jnp.where(x == 0, near, jnp.where(x == end_x, far, middle))
            value = inv * f_r[plane(x), :] + jnp.where(inv > 0.0, coarse, 0.0)
            if beta is not None:
                value = value + beta * f_d[plane(x), :]
            f_d[plane(x), :] = value
            return 0

        lax.fori_loop(0, 7 * cap_x + 1, update, 0)

    def apply_operator():
        def along_x(e, carried):
            values = [f_d[plane(7 * e + c), :] for c in range(8)]
            sums = [values[c] + values[7 - c] for c in range(4)]
            gaps = [values[c] - values[7 - c] for c in range(4)]
            scale = e_px[plane(e + 1), :]
            results = [None] * 8
            for b in range(4):
                even = sum(float(0.5 * (STIFF[b, c] + STIFF[b, 7 - c])) * sums[c] for c in range(4))
                odd = sum(float(0.5 * (STIFF[b, c] - STIFF[b, 7 - c])) * gaps[c] for c in range(4))
                results[b] = scale * (even + odd)
                results[7 - b] = scale * (even - odd)
            f_im[plane(7 * e), :] = carried + results[0]
            for b in range(1, 7):
                f_im[plane(7 * e + b), :] = results[b]
            return results[7]

        carried = lax.fori_loop(0, cap_x, along_x, zero_plane)
        f_im[plane(7 * cap_x), :] = carried

        def along_rest(i, product):
            rows = pl.ds(pl.multiple_of(i * chunk, chunk), chunk)
            value = f_d[rows, :]
            high = value.astype(jnp.bfloat16)
            low = (value - high.astype(jnp.float32)).astype(jnp.bfloat16)
            deep = jnp.dot(
                jnp.concatenate([high, low, high], axis=1),
                vertical_ref[...],
                preferred_element_type=jnp.float32,
            )
            wide = jnp.dot(
                across_ref[...],
                jnp.concatenate([high, low, high], axis=0),
                preferred_element_type=jnp.float32,
            )
            image = f_im[rows, :] + f_mass[rows, :] * value
            image = image + f_ya[rows, :] * wide[0:chunk] + f_yb[rows, :] * wide[chunk:]
            image = image + f_za[rows, :] * deep[:, 0:LANES] + f_zb[rows, :] * deep[:, LANES:]
            f_im[rows, :] = image
            return product + jnp.sum((value * image).reshape(chunk // 8, 8, LANES), axis=0)

        product = lax.fori_loop(0, chunks, along_rest, jnp.zeros((8, LANES), jnp.float32))
        return total(product)

    step0 = reduce_start(0, f_r)
    del step0
    halo_finish(1, f_inv, diagonal_copies)

    def invert(x, value):
        diagonal = f_inv[plane(x), :]
        inverse = jnp.where(diagonal > 0.0, 1.0 / jnp.where(diagonal > 0.0, diagonal, 1.0), 0.0)
        f_inv[plane(x), :] = inverse
        weighed = inverse * share_row * share_x(x)
        f_wid[plane(x), :] = weighed
        resid = f_r[plane(x), :]
        f_sol[plane(x), :] = zero_plane
        return value + weighed * resid * resid

    jacobi = total(lax.fori_loop(0, 7 * cap_x + 1, invert, zero_plane))
    sums = reduce_finish(0, [jacobi])
    jacobi = pick(sums, 0)
    t_now[...] = recv3[0, :, 0:groups, :]
    rho = jacobi + total(jnp.sum(t_now[...] * t_now[...], axis=0))
    copies = coarse_start(0)
    next_direction(0, copies, None)

    for i in range(ITERS):
        curvature = apply_operator()
        image_copies = halo_start(2 + i, f_im)
        if i + 1 < ITERS:
            halo_finish(2 + i, f_im, image_copies)
            reduce_start(i + 1, f_im)

            def dots(x, values):
                image = f_im[plane(x), :]
                weighed = f_wid[plane(x), :] * image
                return (values[0] + weighed * f_r[plane(x), :], values[1] + weighed * image)

            cross, square = lax.fori_loop(0, 7 * cap_x + 1, dots, (zero_plane, zero_plane))
            sums = reduce_finish(i + 1, [curvature, total(cross), total(square)])
            step = rho / pick(sums, 0)
            cross, square = pick(sums, 1), pick(sums, 2)
            jacobi = jacobi - 2.0 * step * cross + step * step * square
            for k in range(nx):
                t_now[k] = t_now[k] - step * recv3[i + 1, k, 0:groups, :]
            rho_next = jacobi + total(jnp.sum(t_now[...] * t_now[...], axis=0))
            copies = coarse_start(i + 1)

            def advance(x, _):
                f_sol[plane(x), :] = f_sol[plane(x), :] + step * f_d[plane(x), :]
                f_r[plane(x), :] = f_r[plane(x), :] - step * f_im[plane(x), :]
                return 0

            lax.fori_loop(0, 7 * cap_x + 1, advance, 0)
            next_direction(i + 1, copies, rho_next / rho)
            rho = rho_next
        else:
            last_s[...] = jnp.broadcast_to(curvature, (1, LANES))

            def send_last(o, _):
                peer = lax.rem(q + o, ny)
                remote(last_s, last_r.at[q], l_send.at[0], l_recv.at[0], (p, peer)).start()
                return 0

            lax.fori_loop(1, ny, send_last, 0)
            last_r[q] = last_s[...]
            halo_finish(2 + i, f_im, image_copies)
            wait_in(last_r, ny - 1, l_send.at[0], l_recv.at[0], beside(0, 1))
            last_s3[...] = jnp.sum(last_r[...], axis=0)

            def send_end(o, _):
                peer = lax.rem(p + o, nx)
                remote(last_s3, last_r3.at[p], l_send.at[1], l_recv.at[1], (peer, q)).start()
                return 0

            lax.fori_loop(1, nx, send_end, 0)
            last_r3[p] = last_s3[...]
            wait_in(last_r3, nx - 1, l_send.at[1], l_recv.at[1], beside(1, 0))
            step = rho / jnp.sum(last_r3[...], axis=0)
            wait_out(last_r, ny - 1, l_send.at[0], l_recv.at[0], beside(0, 1))
            wait_out(last_r3, nx - 1, l_send.at[1], l_recv.at[1], beside(1, 0))

    def finish(x, _):
        f_sol[plane(x), :] = f_sol[plane(x), :] + step * f_d[plane(x), :]
        f_r[plane(x), :] = f_r[plane(x), :] - step * f_im[plane(x), :]
        return 0

    lax.fori_loop(0, 7 * cap_x + 1, finish, 0)

    def put(source, target, x, value):
        last = high_row(value)
        rows = value[0:slots_y, :]
        rows = jnp.where(row < end_y, rows, jnp.where(row == slots_y - 1, last, 0.0))
        target[x] = rows

    for source, target in ((f_sol, solution_ref), (f_r, residual_ref)):

        def write(x, _):
            put(source, target, x, jnp.where(x < end_x, source[plane(x), :], 0.0))
            return 0

        lax.fori_loop(0, slots_x - 1, write, 0)
        put(source, target, slots_x - 1, high_plane(source))


def body(nx, ny, right_side, diffusion, kappa, widths_x, widths_y, factor):
    cap_x, cap_y, layers = diffusion.shape
    slots_x, slots_y, depth = right_side.shape
    groups = factor.shape[1] // (nx * LANES)
    f32 = jnp.float32
    smem = pl.BlockSpec(memory_space=pltpu.SMEM)
    vmem = pl.BlockSpec(memory_space=pltpu.VMEM)
    tall = cap_x * ROWS
    field = pltpu.VMEM((PLANES * ROWS, LANES), f32)
    dma = pltpu.SemaphoreType.DMA
    scratch = [field] * 11 + [
        pltpu.VMEM((tall + 2 * ROWS, LANES), f32),
        pltpu.VMEM((tall + 2 * ROWS, 3 * LANES), f32),
        pltpu.VMEM((tall + 2 * ROWS, LANES), f32),
        pltpu.VMEM((tall + 2 * ROWS, LANES), f32),
        pltpu.VMEM((LANES, LANES), f32),
        pltpu.VMEM((LANES, LANES), f32),
        pltpu.VMEM((nx, groups, LANES), f32),
    ]
    halos = 2 + ITERS
    for _ in range(2):
        scratch += [
            pltpu.VMEM((halos, 2, ROWS, LANES), f32),
            pltpu.VMEM((halos, 2, PLANES, LANES), f32),
            pltpu.VMEM((halos, 4, 8, LANES), f32),
        ]
    scratch += [
        pltpu.VMEM((ITERS, 8, LANES), f32),
        pltpu.VMEM((ITERS, 8, 8, LANES), f32),
        pltpu.VMEM((ITERS, nx, groups, LANES), f32),
        pltpu.VMEM((ITERS, nx, groups, LANES), f32),
        pltpu.VMEM((ITERS, groups + 1, LANES), f32),
        pltpu.VMEM((ITERS, ny, groups + 1, LANES), f32),
        pltpu.VMEM((ITERS, groups + 1, LANES), f32),
        pltpu.VMEM((ITERS, nx, groups + 1, LANES), f32),
        pltpu.VMEM((1, LANES), f32),
        pltpu.VMEM((ny, 1, LANES), f32),
        pltpu.VMEM((1, LANES), f32),
        pltpu.VMEM((nx, 1, LANES), f32),
        dma((halos, 8)), dma((halos, 8)), dma((ITERS, 8)), dma((ITERS, 8)),
        dma((ITERS, 3)), dma((ITERS, 3)), dma((2,)), dma((2,)),
    ]
    shape = jax.ShapeDtypeStruct(right_side.shape, f32)
    constants = [jnp.asarray(table) for table in tables(cap_x, cap_y, layers)]
    return pl.pallas_call(
        functools.partial(kernel, nx, ny, cap_x, cap_y, layers),
        out_shape=(shape, shape),
        in_specs=[smem, smem] + [vmem] * 9,
        out_specs=(vmem, vmem),
        scratch_shapes=scratch,
        compiler_params=pltpu.CompilerParams(
            collective_id=0, has_side_effects=True, vmem_limit_bytes=48 * 1024 * 1024
        ),
    )(widths_x, widths_y, right_side, diffusion, kappa, factor, *constants)


def solution(mesh):
    nx, ny = mesh.shape["gx"], mesh.shape["gy"]
    in_specs = (
        P("gx", "gy", None),
        P("gx", "gy", None),
        P("gx", "gy", None),
        P("gx"),
        P("gy"),
        P(("gx", "gy"), None),
    )
    out_specs = (P("gx", "gy", None), P("gx", "gy", None))
    return jax.shard_map(
        functools.partial(body, nx, ny),
        mesh=mesh,
        in_specs=in_specs,
        out_specs=out_specs,
        check_vma=False,
    )
```

```python
import functools

import jax
import jax.numpy as jnp
import ml_dtypes
import numpy as np
from jax import lax
from jax.experimental import pallas as pl
from jax.experimental.pallas import tpu as pltpu
from jax.sharding import PartitionSpec as P

ITERS = 3
HIGHEST = lax.Precision.HIGHEST
MESH = pl.DeviceIdType.MESH
LANES = 128
ROWS = 32
PLANES = 48
BLOCK = 4
DIRECTIONS = [(1, 0), (-1, 0), (0, 1), (0, -1), (1, 1), (1, -1), (-1, 1), (-1, -1)]


def gll_weights():
    return np.array(
        [
            1.0 / 28.0,
            0.2107042271435061,
            0.3411226924835044,
            0.4124587946587038,
            0.4124587946587038,
            0.3411226924835044,
            0.2107042271435061,
            1.0 / 28.0,
        ]
    )


def gll_derivative():
    points = np.array(
        [
            -1.0,
            -0.8717401485096066,
            -0.5917001814331423,
            -0.2092992179024789,
            0.2092992179024789,
            0.5917001814331423,
            0.8717401485096066,
            1.0,
        ]
    )
    identity = np.eye(8) > 0
    spacing = np.where(identity, 1.0, points[:, None] - points[None, :])
    barycentric = 1.0 / np.prod(spacing, axis=1)
    matrix = np.where(identity, 0.0, barycentric[None, :] / barycentric[:, None] / spacing)
    return np.where(identity, -np.sum(matrix, axis=1)[:, None], matrix)


WEIGHTS = gll_weights()
STIFF = gll_derivative().T @ np.diag(WEIGHTS) @ gll_derivative()


def split(matrix):
    high = matrix.astype(ml_dtypes.bfloat16)
    low = (matrix - high.astype(np.float64)).astype(ml_dtypes.bfloat16)
    return high, low


def band(cells, size):
    first, second = np.zeros((size, size)), np.zeros((size, size))
    for e in range(cells):
        for b in range(7):
            first[7 * e + b, 7 * e : 7 * e + 8] = STIFF[b]
        second[7 * e + 7, 7 * e : 7 * e + 8] = STIFF[7]
    return first, second


def tables(cap_x, cap_y, layers):
    first, second = band(layers, LANES)
    high, low = split(np.concatenate([first, second], axis=0).T)
    vertical = np.concatenate([high, high, low], axis=0)
    first, second = band(cap_y, ROWS)
    stacked = np.concatenate([np.kron(np.eye(4), first), np.kron(np.eye(4), second)], axis=0)
    high, low = split(stacked)
    across = np.concatenate([high, high, low], axis=1)
    depth = np.zeros((LANES, 3 * LANES))
    for h in range(layers):
        depth[h, 7 * h : 7 * h + 8] = WEIGHTS
        depth[h, LANES + 7 * h : LANES + 7 * h + 7] = 1.0
        depth[h, 2 * LANES + 7 * h + 7] = 1.0
    weigh, pick, ends = np.zeros((ROWS, 8)), np.zeros((ROWS, 8)), np.zeros((ROWS, 8))
    for f in range(cap_y):
        weigh[7 * f : 7 * f + 8, f] = WEIGHTS
        pick[7 * f : 7 * f + 7, f] = 1.0
        ends[7 * f + 7, f] = 1.0
    unit = np.eye(cap_x)
    widen = np.concatenate([np.kron(unit, weigh), np.kron(unit, pick), np.kron(unit, ends)], axis=0)
    widen = np.pad(widen, ((0, 0), (0, LANES - widen.shape[1])))
    factor = np.zeros((ROWS + 8, LANES))
    factor[: 7 * cap_y] = STIFF[np.arange(7 * cap_y) % 7, np.arange(7 * cap_y) % 7][:, None]
    factor[ROWS:, : 7 * layers] = STIFF[np.arange(7 * layers) % 7, np.arange(7 * layers) % 7][None, :]
    return (
        vertical,
        across,
        depth.astype(np.float32),
        widen.astype(np.float32),
        factor.astype(np.float32),
    )


def plane(x):
    return pl.ds(pl.multiple_of(x * ROWS, ROWS), ROWS)


def total(values):
    return jnp.sum(values, axis=(0, 1), keepdims=True)


def iota(shape, dim):
    return lax.broadcasted_iota(jnp.int32, shape, dim)


def pieces(values):
    first = values.astype(jnp.bfloat16)
    rest = values - first.astype(jnp.float32)
    second = rest.astype(jnp.bfloat16)
    third = (rest - second.astype(jnp.float32)).astype(jnp.bfloat16)
    return [first, second, third]


def exact_dot(values, chosen):
    rows = values.shape[0]
    result = jnp.dot(
        jnp.concatenate(pieces(values), axis=0), chosen, preferred_element_type=jnp.float32
    )
    return result[0:rows] + result[rows : 2 * rows] + result[2 * rows : 3 * rows]


def kernel(
    nx, ny, cap_x, cap_y, layers, bx, by,
    wx_ref, wy_ref, load_any, diff_any, kappa_any, factor_any,
    vertical_any, across_any, depth_any, widen_any, coefficient_any,
    solution_ref, residual_ref,
    load_ref, diff_ref, kappa_ref,
    vertical_ref, across_ref, depth_ref, widen_ref, coefficient_ref,
    f_z, f_im, f_w, f_d, f_r, f_sol, f_inv, f_share, f_mass, f_ya, f_yb, f_za, f_zb,
    e_px, e_big, e_ya, e_yb, squares, sq_kappa,
    rows_x, gather_map, spread_map,
    halo_sx, halo_sy, halo_sc, halo_rx, halo_ry, halo_rc,
    grid_s, grid_r, chunk_s, chunk_r, back_s, back_r, last_s, last_r, end_s, end_r,
    in_sem, own_sem, x_send, x_recv, ring_send, ring_recv,
    h_send, h_recv, r_send, r_recv, l_send, l_recv,
):
    p, q = lax.axis_index("gx"), lax.axis_index("gy")
    wx, wy = wx_ref[0], wy_ref[0]
    groups = chunk_s.shape[1] - 1
    width = groups * LANES
    end_x, end_y = 7 * wx, 7 * wy
    near, far = bx * by, (nx // bx) * (ny // by)
    ax, ay = nx // bx, ny // by
    bi, bj, ai, aj = lax.rem(p, bx), lax.rem(q, by), p // bx, q // by
    mine, block_id = bi * by + bj, ai * ay + aj

    def beside(dx, dy):
        return (lax.rem(p + dx + nx, nx), lax.rem(q + dy + ny, ny))

    def in_block(index):
        return (ai * bx + index // by, aj * by + lax.rem(index, by))

    def across(index):
        return (index // ay * bx + bi, lax.rem(index, ay) * by + bj)

    barrier = pltpu.get_barrier_semaphore()

    def greet(device):
        pl.semaphore_signal(barrier, inc=1, device_id=device, device_id_type=MESH)

    def greet_near(o, _):
        greet(in_block(lax.rem(mine + o, near)))
        return 0

    def greet_far(o, _):
        greet(across(lax.rem(block_id + o, far)))
        return 0

    lax.fori_loop(1, near, greet_near, 0)
    lax.fori_loop(1, far, greet_far, 0)
    for dx, dy in DIRECTIONS:
        greet(beside(dx, dy))

    arrivals = []
    for i, (source, target) in enumerate((
        (diff_any, diff_ref), (kappa_any, kappa_ref), (depth_any, depth_ref),
        (widen_any, widen_ref), (coefficient_any, coefficient_ref), (load_any, load_ref),
        (vertical_any, vertical_ref), (across_any, across_ref),
    )):
        copy = pltpu.make_async_copy(source, target, in_sem.at[i])
        copy.start()
        arrivals.append(copy)

    def remote(source, target, send, recv, device):
        return pltpu.make_async_remote_copy(
            src_ref=source,
            dst_ref=target,
            send_sem=send,
            recv_sem=recv,
            device_id=device,
            device_id_type=MESH,
        )

    def columns(index):
        return pl.ds(pl.multiple_of(index * width, LANES), width)

    def rows_of(j):
        return pl.ds(pl.multiple_of((j + 1) * 16, 16), 16)

    own_rows = pltpu.make_async_copy(
        factor_any.at[:, columns(mine)], rows_x.at[bi + 1, rows_of(bj), :], own_sem.at[0]
    )
    own_rows.start()

    def flag(condition):
        return jnp.where(condition, 1.0, 0.0).astype(jnp.float32)

    has_left, has_right = flag(p > 0), flag(p < nx - 1)
    has_below, has_above = flag(q > 0), flag(q < ny - 1)

    pl.semaphore_wait(barrier, near + far - 2 + len(DIRECTIONS))

    def scatter_copy(o):
        peer = lax.rem(mine + o, near)
        return remote(
            factor_any.at[:, columns(peer)],
            rows_x.at[bi + 1, rows_of(bj), :],
            x_send.at[o],
            x_recv.at[o],
            in_block(peer),
        )

    def scatter(o, _):
        scatter_copy(o).start()
        return 0

    lax.fori_loop(1, near, scatter, 0)

    squares[...] = jnp.zeros_like(squares)
    sq_kappa[...] = jnp.zeros_like(sq_kappa)
    for copy in arrivals[0:5]:
        copy.wait()
    inside = iota((cap_y, layers), 0) < wy
    for e in range(cap_x):
        keep = inside & (e < wx)
        squares[8 * e : 8 * e + cap_y, 0:layers] = jnp.where(keep, diff_ref[e], 0.0)
        sq_kappa[8 * e : 8 * e + cap_y, 0:layers] = jnp.where(keep, kappa_ref[e], 0.0)
    deep = jnp.dot(squares[...], depth_ref[...], precision=HIGHEST, preferred_element_type=jnp.float32)
    deep_kappa = jnp.dot(
        sq_kappa[...], depth_ref[:, 0:LANES], precision=HIGHEST, preferred_element_type=jnp.float32
    )
    tall = cap_x * ROWS
    big = jnp.dot(
        widen_ref[0:tall, :],
        jnp.concatenate([deep, deep_kappa], axis=1),
        precision=HIGHEST,
        preferred_element_type=jnp.float32,
    )
    both = jnp.dot(
        widen_ref[tall : 3 * tall, :],
        deep[:, 0:LANES],
        precision=HIGHEST,
        preferred_element_type=jnp.float32,
    )
    zero_plane = jnp.zeros((ROWS, LANES), jnp.float32)
    for ref in (e_px, e_ya, e_yb):
        ref[0:ROWS, :] = zero_plane
        ref[tall + ROWS : tall + 2 * ROWS, :] = zero_plane
    for place in (0, tall + ROWS):
        e_big[place : place + ROWS, :] = jnp.zeros((ROWS, 3 * LANES), jnp.float32)
    e_px[ROWS : ROWS + tall, :] = big[:, 0:LANES]
    e_big[ROWS : ROWS + tall, :] = big[:, LANES : 4 * LANES]
    e_ya[ROWS : ROWS + tall, :] = both[0:tall]
    e_yb[ROWS : ROWS + tall, :] = both[tall : 2 * tall]

    fields = (f_z, f_im, f_r, f_inv, f_mass, f_ya, f_yb, f_za, f_zb)
    for ref in fields:
        for x in range(7 * cap_x, PLANES):
            ref[x * ROWS : (x + 1) * ROWS, :] = zero_plane

    sources = (
        (f_za, e_big, 0), (f_zb, e_big, 1), (f_mass, e_big, 2), (f_ya, e_ya, 0), (f_yb, e_yb, 0),
    )
    row_factor = coefficient_ref[0:ROWS, :]
    depth_factor = coefficient_ref[ROWS : ROWS + 1, :]
    corner = float(STIFF[7, 7])

    def fill_plane(x, e, b):
        values = []
        for target, source, lane in sources:
            lanes = slice(lane * LANES, (lane + 1) * LANES)
            value = float(WEIGHTS[b]) * source[plane(e + 1), lanes]
            if b == 0:
                value = value + float(WEIGHTS[7]) * source[plane(e), lanes]
            target[plane(x), :] = value
            values.append(value)
        za, zb, mass, ya, yb = values
        diagonal = mass + ya * row_factor + yb * corner + za * depth_factor + zb * corner
        diagonal = diagonal + float(STIFF[b, b]) * e_px[plane(e + 1), :]
        if b == 0:
            diagonal = diagonal + float(STIFF[7, 7]) * e_px[plane(e), :]
        f_inv[plane(x), :] = diagonal

    def fill(e, _):
        for b in range(7):
            fill_plane(7 * e + b, e, b)
        return 0

    lax.fori_loop(0, cap_x, fill, 0)
    fill_plane(7 * cap_x, cap_x, 0)

    slots_x, slots_y = load_ref.shape[0], load_ref.shape[1]
    row = iota((slots_y, LANES), 0)
    real = iota((slots_y, LANES), 1) <= 7 * layers
    f_r[...] = jnp.zeros_like(f_r)
    arrivals[5].wait()

    def take(x, _):
        value = jnp.where(x < end_x, load_ref[x], jnp.where(x == end_x, load_ref[slots_x - 1], 0.0))
        last = value[slots_y - 1 : slots_y, :]
        value = jnp.where(row < end_y, value, jnp.where(row == end_y, last, 0.0))
        f_r[pl.ds(pl.multiple_of(x * ROWS, ROWS), slots_y), :] = jnp.where(real, value, 0.0)
        return 0

    lax.fori_loop(0, slots_x, take, 0)

    def high_plane(ref):
        value = jnp.zeros((ROWS, LANES), jnp.float32)
        for j in range(1, cap_x + 1):
            value = value + jnp.where(wx == j, ref[7 * j * ROWS : (7 * j + 1) * ROWS, :], 0.0)
        return value

    def side(j):
        return pl.ds(7 * j, PLANES, stride=ROWS)

    def high_row(plane_value):
        value = jnp.zeros((1, LANES), jnp.float32)
        for j in range(1, cap_y + 1):
            value = value + jnp.where(wy == j, plane_value[7 * j : 7 * j + 1, :], 0.0)
        return value

    def halo_copies(h):
        copies = []
        for k, (dx, dy) in enumerate(DIRECTIONS):
            if dy == 0:
                slot = (h, 0 if dx > 0 else 1)
                source, target = halo_sx.at[slot], halo_rx.at[slot]
            elif dx == 0:
                slot = (h, 0 if dy > 0 else 1)
                source, target = halo_sy.at[slot], halo_ry.at[slot]
            else:
                source, target = halo_sc.at[h, k - 4], halo_rc.at[h, k - 4]
            copies.append(remote(source, target, h_send.at[h, k], h_recv.at[h, k], beside(dx, dy)))
        return copies

    def halo_start(h, ref):
        low, high = ref[0:ROWS, :], high_plane(ref)
        halo_sx[h, 0] = high
        halo_sx[h, 1] = low
        above = jnp.zeros((PLANES, LANES), jnp.float32)
        for j in range(1, cap_y + 1):
            above = above + jnp.where(wy == j, ref[side(j), :], 0.0)
        halo_sy[h, 0] = above
        halo_sy[h, 1] = ref[side(0), :]
        rows = (high_row(high), high[0:1, :], high_row(low), low[0:1, :])
        for k, value in enumerate(rows):
            halo_sc[h, k] = jnp.broadcast_to(value, (8, LANES))
        copies = halo_copies(h)
        for copy in copies:
            copy.start()
        return copies

    place = iota((PLANES, LANES), 0)

    def halo_finish(h, ref, copies):
        for copy in copies:
            copy.wait()
        ref[0:ROWS, :] = ref[0:ROWS, :] + has_left * halo_rx[h, 0]
        from_right = has_right * halo_rx[h, 1]
        for j in range(1, cap_x + 1):
            rows = slice(7 * j * ROWS, (7 * j + 1) * ROWS)
            ref[rows, :] = ref[rows, :] + jnp.where(wx == j, from_right, 0.0)

        def line(side_value, first, second):
            side_value = side_value + jnp.where(place == 0, has_left * first[0:1, :], 0.0)
            return side_value + jnp.where(place == end_x, has_right * second[0:1, :], 0.0)

        below = has_below * line(halo_ry[h, 0], halo_rc[h, 0], halo_rc[h, 2])
        above = has_above * line(halo_ry[h, 1], halo_rc[h, 1], halo_rc[h, 3])
        ref[side(0), :] = ref[side(0), :] + below
        for j in range(1, cap_y + 1):
            ref[side(j), :] = ref[side(j), :] + jnp.where(wy == j, above, 0.0)

    deep_node, deep_lane = iota((LANES, LANES), 0), iota((LANES, LANES), 1)
    for dy in (-1, 0, 1):
        part = slice((dy + 1) * LANES, (dy + 2) * LANES)
        start = (bj + 1 + dy) * 16
        gather_map[part, :] = flag(deep_lane == start + deep_node // 8).astype(jnp.bfloat16)
        spread_map[:, part] = flag(deep_node == start + deep_lane // 8).astype(jnp.bfloat16)
    grid_row = iota((8, LANES), 0)
    row32 = iota((ROWS, LANES), 0)
    chunk = 4 * ROWS
    chunks = (7 * cap_x + 4) // 4

    def coarse_sums(ref):
        def add(i, value):
            return value + jnp.sum(
                ref[pl.ds(pl.multiple_of(i * chunk, chunk), chunk), :].reshape(4, ROWS, LANES), axis=0
            )

        middle = lax.fori_loop(0, chunks, add, zero_plane)
        low, high = 0.5 * has_left * ref[0:ROWS, :], 0.5 * has_right * high_plane(ref)
        sums = [jnp.zeros((8, LANES), jnp.float32)] * 3
        for dx, value in ((-1, low), (0, middle - low - high), (1, high)):
            below = 0.5 * has_below * value[0:1, :]
            above = 0.5 * has_above * high_row(value)
            centre = jnp.sum(value, axis=0, keepdims=True) - below - above
            for k, profile in enumerate((below, centre, above)):
                sums[k] = sums[k] + jnp.where(grid_row == bi + 1 + dx, profile, 0.0)
        return exact_dot(jnp.concatenate(sums, axis=1), gather_map[...])

    def wait_in(buffer, count, send, recv):
        part = buffer.at[pl.ds(0, count)]
        remote(part, part, send, recv, beside(1, 0)).wait_recv()

    def wait_out(buffer, count, send, recv):
        part = buffer.at[pl.ds(0, count)]
        remote(part, part, send, recv, beside(1, 0)).wait_send()

    def exchange_start(source, target, count, me, device, send, recv):
        def go(o, _):
            remote(source, target.at[me], send, recv, device(lax.rem(me + o, count))).start()
            return 0

        lax.fori_loop(1, count, go, 0)
        target[me] = source[...]

    def reduce_start(a, ref):
        grid_s[a] = coarse_sums(ref)
        exchange_start(
            grid_s.at[a], grid_r.at[a], near, mine, in_block, r_send.at[a, 0], r_recv.at[a, 0]
        )

    lane = iota((1, LANES), 1)

    def scalar_row(values):
        result = jnp.zeros((1, LANES), jnp.float32)
        for i, value in enumerate(values):
            result = jnp.where(lane == i, value, result)
        return result

    def pick(values, i):
        return total(jnp.where(lane == i, values, 0.0))

    grid_rows, grid_lanes = bx + 2, (by + 2) * 16

    def reduce_middle(a, scalars):
        wait_in(grid_r.at[a], near - 1, r_send.at[a, 0], r_recv.at[a, 0])
        turned = jnp.sum(grid_r[a], axis=0).T
        value = jnp.zeros((8, width), jnp.float32)
        for i in range(grid_rows):
            product = rows_x[i] * turned[0:grid_lanes, i : i + 1]
            value = value + jnp.sum(product.reshape(grid_lanes // 8, 8, width), axis=0)
        value = jnp.sum(value, axis=0, keepdims=True)
        for g in range(groups):
            chunk_s[a, g : g + 1, :] = value[:, g * LANES : (g + 1) * LANES]
        chunk_s[a, groups : groups + 1, :] = scalar_row(scalars)
        exchange_start(
            chunk_s.at[a], chunk_r.at[a], far, block_id, across, r_send.at[a, 1], r_recv.at[a, 1]
        )

    def reduce_finish(a, extra):
        wait_in(chunk_r.at[a], far - 1, r_send.at[a, 1], r_recv.at[a, 1])
        sums = jnp.sum(chunk_r[a], axis=0)
        through = sums[0:groups, :]
        turned = jnp.zeros((grid_lanes, LANES), jnp.float32)
        wide_lane = iota((grid_lanes, LANES), 1)
        for i in range(grid_rows):
            product = rows_x[i, :, 0:LANES] * through[0:1, :]
            for g in range(1, groups):
                product = product + rows_x[i, :, g * LANES : (g + 1) * LANES] * through[g : g + 1, :]
            turned = jnp.where(wide_lane == i, jnp.sum(product, axis=1, keepdims=True), turned)
        turned = jnp.concatenate(
            [turned, jnp.zeros((LANES - grid_lanes, LANES), jnp.float32)], axis=0
        )
        scalars = sums[groups : groups + 1, :]
        if extra is not None:
            scalars = jnp.where(lane == 8, extra, scalars)
        back_s[a] = jnp.where(grid_row == 7, scalars, turned.T[0:8, :])
        exchange_start(
            back_s.at[a], back_r.at[a], near, mine, in_block, r_send.at[a, 2], r_recv.at[a, 2]
        )
        wait_in(back_r.at[a], near - 1, r_send.at[a, 2], r_recv.at[a, 2])
        grid = jnp.sum(back_r[a], axis=0)
        wait_out(grid_r.at[a], near - 1, r_send.at[a, 0], r_recv.at[a, 0])
        wait_out(chunk_r.at[a], far - 1, r_send.at[a, 1], r_recv.at[a, 1])
        wait_out(back_r.at[a], near - 1, r_send.at[a, 2], r_recv.at[a, 2])
        return grid, grid[7:8, :], through

    def coarse_planes(grid):
        deep_values = exact_dot(grid, spread_map[...])

        def spread(dx):
            line = jnp.sum(jnp.where(iota((8, 3 * LANES), 0) == bi + 1 + dx, deep_values, 0.0), axis=0, keepdims=True)
            below, centre, above = (line[:, k * LANES : (k + 1) * LANES] for k in range(3))
            value = jnp.where(row32 == 0, centre + 0.5 * has_below * (below - centre), centre)
            return jnp.where(row32 == end_y, value + 0.5 * has_above * (above - centre), value)

        middle = spread(0)
        first = middle + 0.5 * has_left * (spread(-1) - middle)
        second = middle + 0.5 * has_right * (spread(1) - middle)
        return first, middle, second

    def coarse_at(x, planes):
        first, middle, second = planes
        return jnp.where(x == 0, first, jnp.where(x == end_x, second, middle))

    def apply_operator():
        def along_x(e, carried):
            values = [f_z[plane(7 * e + c), :] for c in range(8)]
            sums = [values[c] + values[7 - c] for c in range(4)]
            gaps = [values[c] - values[7 - c] for c in range(4)]
            scale = e_px[plane(e + 1), :]
            results = [None] * 8
            for b in range(4):
                even = sum(float(0.5 * (STIFF[b, c] + STIFF[b, 7 - c])) * sums[c] for c in range(4))
                odd = sum(float(0.5 * (STIFF[b, c] - STIFF[b, 7 - c])) * gaps[c] for c in range(4))
                results[b] = scale * (even + odd)
                results[7 - b] = scale * (even - odd)
            f_im[plane(7 * e), :] = carried + results[0]
            for b in range(1, 7):
                f_im[plane(7 * e + b), :] = results[b]
            return results[7]

        carried = lax.fori_loop(0, cap_x, along_x, zero_plane)
        f_im[plane(7 * cap_x), :] = carried

        def along_rest(i, product):
            rows = pl.ds(pl.multiple_of(i * chunk, chunk), chunk)
            value = f_z[rows, :]
            high = value.astype(jnp.bfloat16)
            low = (value - high.astype(jnp.float32)).astype(jnp.bfloat16)
            deep = jnp.dot(
                jnp.concatenate([high, low, high], axis=1),
                vertical_ref[...],
                preferred_element_type=jnp.float32,
            )
            wide = jnp.dot(
                across_ref[...],
                jnp.concatenate([high, low, high], axis=0),
                preferred_element_type=jnp.float32,
            )
            image = f_im[rows, :] + f_mass[rows, :] * value
            image = image + f_ya[rows, :] * wide[0:chunk] + f_yb[rows, :] * wide[chunk:]
            image = image + f_za[rows, :] * deep[:, 0:LANES] + f_zb[rows, :] * deep[:, LANES:]
            f_im[rows, :] = image
            return product + jnp.sum((value * image).reshape(chunk // 8, 8, LANES), axis=0)

        product = lax.fori_loop(0, chunks, along_rest, jnp.zeros((8, LANES), jnp.float32))
        return total(product)

    reduce_start(0, f_r)
    load_copies = halo_start(0, f_r)
    diagonal_copies = halo_start(1, f_inv)

    own_rows.wait()

    def scatter_wait(o, _):
        scatter_copy(o).wait()
        return 0

    lax.fori_loop(1, near, scatter_wait, 0)
    spans = {1: (slice(bx, bx + 1), slice(0, 1)), -1: (slice(1, 2), slice(bx + 1, bx + 2))}
    spans[0] = (slice(1, bx + 1), slice(1, bx + 1))
    across_spans = {1: (by, 0, 1), -1: (1, by + 1, 1), 0: (1, 1, by)}
    ring = []
    for k, (dx, dy) in enumerate(DIRECTIONS):
        (source_x, target_x), (source_y, target_y, count) = spans[dx], across_spans[dy]
        copy = remote(
            rows_x.at[source_x, pl.ds(source_y * 16, count * 16), :],
            rows_x.at[target_x, pl.ds(target_y * 16, count * 16), :],
            ring_send.at[k],
            ring_recv.at[k],
            beside(dx * bx, dy * by),
        )
        copy.start()
        ring.append(copy)

    halo_finish(0, f_r, load_copies)
    halo_finish(1, f_inv, diagonal_copies)
    share_low = jnp.where(row32 == 0, 1.0 - 0.5 * has_below, 1.0)
    share_row = jnp.where(row32 == end_y, 1.0 - 0.5 * has_above, share_low)

    def share_x(x):
        low = jnp.where(x == 0, 1.0 - 0.5 * has_left, 1.0)
        return jnp.where(x == end_x, 1.0 - 0.5 * has_right, low)

    def invert(x, value):
        diagonal = f_inv[plane(x), :]
        inverse = jnp.where(diagonal > 0.0, 1.0 / jnp.where(diagonal > 0.0, diagonal, 1.0), 0.0)
        f_inv[plane(x), :] = inverse
        share = jnp.where(diagonal > 0.0, share_row * share_x(x), 0.0)
        f_share[plane(x), :] = share
        resid = f_r[plane(x), :]
        f_sol[plane(x), :] = zero_plane
        f_w[plane(x), :] = zero_plane
        f_d[plane(x), :] = zero_plane
        return value + share * inverse * resid * resid

    planes = 7 * cap_x + 1
    jacobi = total(lax.fori_loop(0, planes, invert, zero_plane))
    for copy in ring:
        copy.wait()
    for copy in arrivals[6:]:
        copy.wait()
    reduce_middle(0, [])
    grid, _, through = reduce_finish(0, None)
    coarse = coarse_planes(grid)

    def begin(x, _):
        inverse = f_inv[plane(x), :]
        value = jnp.where(inverse > 0.0, coarse_at(x, coarse), 0.0)
        f_z[plane(x), :] = inverse * f_r[plane(x), :] + value
        return 0

    lax.fori_loop(0, planes, begin, 0)

    cross = jnp.zeros((1, 1), jnp.float32)
    beta, rho, curvature = cross, None, cross
    through_w, grid_w = jnp.zeros_like(through), jnp.zeros_like(grid)

    def scalars_of(values, squared):
        rho_now = pick(values, 2) + squared
        beta_now = jnp.zeros((1, 1), jnp.float32) if rho is None else rho_now / rho
        bent = pick(values, 0) + 2.0 * beta_now * pick(values, 1) + beta_now * beta_now * curvature
        return rho_now, beta_now, bent

    for i in range(ITERS):
        own = apply_operator()
        squared = total(through * through)
        if i + 1 < ITERS:
            reduce_start(i + 1, f_im)
            image_copies = halo_start(2 + i, f_im)
            reduce_middle(i + 1, [own, cross, jacobi])
            halo_finish(2 + i, f_im, image_copies)
            grid_q, values, through_q = reduce_finish(i + 1, squared)
            rho, beta, curvature = scalars_of(values, pick(values, 8))
            step = rho / curvature
            grid_w = grid_q + beta * grid_w
            through_w = through_q + beta * through_w
            grid = grid - step * grid_w
            through = through - step * through_w
            coarse = coarse_planes(grid)

            def advance(x, sums):
                here = plane(x)
                old = f_z[here, :]
                direction = old + beta * f_d[here, :]
                image = f_im[here, :] + beta * f_w[here, :]
                f_d[here, :] = direction
                f_w[here, :] = image
                f_sol[here, :] = f_sol[here, :] + step * direction
                resid = f_r[here, :] - step * image
                f_r[here, :] = resid
                scaled = f_inv[here, :] * resid
                share = f_share[here, :]
                value = scaled + jnp.where(share > 0.0, coarse_at(x, coarse), 0.0)
                f_z[here, :] = value
                return sums[0] + share * scaled * resid, sums[1] + share * value * image

            jacobi, cross = lax.fori_loop(0, planes, advance, (zero_plane, zero_plane))
            jacobi, cross = total(jacobi), total(cross)
        else:
            last_s[...] = scalar_row([own, cross, jacobi])
            exchange_start(last_s, last_r, far, block_id, across, l_send.at[0], l_recv.at[0])
            image_copies = halo_start(2 + i, f_im)
            halo_finish(2 + i, f_im, image_copies)
            wait_in(last_r, far - 1, l_send.at[0], l_recv.at[0])
            end_s[...] = jnp.where(lane == 8, squared, jnp.sum(last_r[...], axis=0))
            exchange_start(end_s, end_r, near, mine, in_block, l_send.at[1], l_recv.at[1])
            wait_in(end_r, near - 1, l_send.at[1], l_recv.at[1])
            values = jnp.sum(end_r[...], axis=0)
            rho, beta, curvature = scalars_of(values, pick(values, 8))
            step = rho / curvature
            wait_out(last_r, far - 1, l_send.at[0], l_recv.at[0])
            wait_out(end_r, near - 1, l_send.at[1], l_recv.at[1])

    def put(target, x, value):
        last = high_row(value)
        rows = value[0:slots_y, :]
        rows = jnp.where(row < end_y, rows, jnp.where(row == slots_y - 1, last, 0.0))
        target[x] = rows

    def finish(x, _):
        here = plane(x)
        found = f_sol[here, :] + step * (f_z[here, :] + beta * f_d[here, :])
        resid = f_r[here, :] - step * (f_im[here, :] + beta * f_w[here, :])
        f_sol[here, :] = found
        f_r[here, :] = resid
        put(solution_ref, x, jnp.where(x < end_x, found, 0.0))
        put(residual_ref, x, jnp.where(x < end_x, resid, 0.0))
        return 0

    lax.fori_loop(0, planes, finish, 0)
    put(solution_ref, slots_x - 1, high_plane(f_sol))
    put(residual_ref, slots_x - 1, high_plane(f_r))


def body(nx, ny, right_side, diffusion, kappa, widths_x, widths_y, factor):
    cap_x, cap_y, layers = diffusion.shape
    bx, by = BLOCK, BLOCK
    near, far = bx * by, (nx // bx) * (ny // by)
    groups = factor.shape[1] // (near * LANES)
    f32, bf16 = jnp.float32, jnp.bfloat16
    smem = pl.BlockSpec(memory_space=pltpu.SMEM)
    vmem = pl.BlockSpec(memory_space=pltpu.VMEM)
    hbm = pl.BlockSpec(memory_space=pltpu.HBM)
    tall = cap_x * ROWS
    dma = pltpu.SemaphoreType.DMA
    constants = [jnp.asarray(table) for table in tables(cap_x, cap_y, layers)]

    def room(*shape, dtype=f32):
        return pltpu.VMEM(shape, dtype)

    scratch = [room(*array.shape, dtype=array.dtype) for array in (right_side, diffusion, kappa)]
    scratch += [room(*array.shape, dtype=array.dtype) for array in constants]
    scratch += [room(PLANES * ROWS, LANES)] * 13
    scratch += [
        room(tall + 2 * ROWS, LANES),
        room(tall + 2 * ROWS, 3 * LANES),
        room(tall + 2 * ROWS, LANES),
        room(tall + 2 * ROWS, LANES),
        room(LANES, LANES),
        room(LANES, LANES),
        room(bx + 2, (by + 2) * 16, groups * LANES),
        room(3 * LANES, LANES, dtype=bf16),
        room(LANES, 3 * LANES, dtype=bf16),
    ]
    halos = 2 + ITERS
    for _ in range(2):
        scratch += [
            room(halos, 2, ROWS, LANES),
            room(halos, 2, PLANES, LANES),
            room(halos, 4, 8, LANES),
        ]
    scratch += [
        room(ITERS, 8, LANES),
        room(ITERS, near, 8, LANES),
        room(ITERS, groups + 1, LANES),
        room(ITERS, far, groups + 1, LANES),
        room(ITERS, 8, LANES),
        room(ITERS, near, 8, LANES),
        room(1, LANES),
        room(far, 1, LANES),
        room(1, LANES),
        room(near, 1, LANES),
        dma((8,)), dma((1,)), dma((near,)), dma((near,)), dma((8,)), dma((8,)),
        dma((halos, 8)), dma((halos, 8)), dma((ITERS, 3)), dma((ITERS, 3)), dma((2,)), dma((2,)),
    ]
    shape = jax.ShapeDtypeStruct(right_side.shape, f32)
    return pl.pallas_call(
        functools.partial(kernel, nx, ny, cap_x, cap_y, layers, bx, by),
        out_shape=(shape, shape),
        in_specs=[smem, smem] + [hbm] * 9,
        out_specs=(vmem, vmem),
        scratch_shapes=scratch,
        compiler_params=pltpu.CompilerParams(
            collective_id=0, has_side_effects=True, vmem_limit_bytes=48 * 1024 * 1024
        ),
    )(widths_x, widths_y, right_side, diffusion, kappa, factor, *constants)


def solution(mesh):
    nx, ny = mesh.shape["gx"], mesh.shape["gy"]
    in_specs = (
        P("gx", "gy", None),
        P("gx", "gy", None),
        P("gx", "gy", None),
        P("gx"),
        P("gy"),
        P(("gx", "gy"), None),
    )
    out_specs = (P("gx", "gy", None), P("gx", "gy", None))
    return jax.shard_map(
        functools.partial(body, nx, ny),
        mesh=mesh,
        in_specs=in_specs,
        out_specs=out_specs,
        check_vma=False,
    )
```

```python
import functools

import jax
import jax.numpy as jnp
import ml_dtypes
import numpy as np
from jax import lax
from jax.experimental import pallas as pl
from jax.experimental.pallas import tpu as pltpu
from jax.sharding import PartitionSpec as P

ITERS = 3
HIGHEST = lax.Precision.HIGHEST
MESH = pl.DeviceIdType.MESH
LANES = 128
ROWS = 32
PLANES = 48
BLOCK = 4
DIRECTIONS = [(1, 0), (-1, 0), (0, 1), (0, -1), (1, 1), (1, -1), (-1, 1), (-1, -1)]


def gll_weights():
    return np.array(
        [
            1.0 / 28.0,
            0.2107042271435061,
            0.3411226924835044,
            0.4124587946587038,
            0.4124587946587038,
            0.3411226924835044,
            0.2107042271435061,
            1.0 / 28.0,
        ]
    )


def gll_derivative():
    points = np.array(
        [
            -1.0,
            -0.8717401485096066,
            -0.5917001814331423,
            -0.2092992179024789,
            0.2092992179024789,
            0.5917001814331423,
            0.8717401485096066,
            1.0,
        ]
    )
    identity = np.eye(8) > 0
    spacing = np.where(identity, 1.0, points[:, None] - points[None, :])
    barycentric = 1.0 / np.prod(spacing, axis=1)
    matrix = np.where(identity, 0.0, barycentric[None, :] / barycentric[:, None] / spacing)
    return np.where(identity, -np.sum(matrix, axis=1)[:, None], matrix)


WEIGHTS = gll_weights()
STIFF = gll_derivative().T @ np.diag(WEIGHTS) @ gll_derivative()


def split(matrix):
    high = matrix.astype(ml_dtypes.bfloat16)
    low = (matrix - high.astype(np.float64)).astype(ml_dtypes.bfloat16)
    return high, low


def band(cells, size):
    first, second = np.zeros((size, size)), np.zeros((size, size))
    for e in range(cells):
        for b in range(7):
            first[7 * e + b, 7 * e : 7 * e + 8] = STIFF[b]
        second[7 * e + 7, 7 * e : 7 * e + 8] = STIFF[7]
    return first, second


def tables(cap_x, cap_y, layers):
    first, second = band(layers, LANES)
    vertical = split(np.concatenate([first, second], axis=0).T)
    first, second = band(cap_y, ROWS)
    stacked = np.concatenate([np.kron(np.eye(4), first), np.kron(np.eye(4), second)], axis=0)
    across = split(stacked)
    depth = np.zeros((LANES, 3 * LANES))
    for h in range(layers):
        depth[h, 7 * h : 7 * h + 8] = WEIGHTS
        depth[h, LANES + 7 * h : LANES + 7 * h + 7] = 1.0
        depth[h, 2 * LANES + 7 * h + 7] = 1.0
    weigh, pick, ends = np.zeros((ROWS, 8)), np.zeros((ROWS, 8)), np.zeros((ROWS, 8))
    for f in range(cap_y):
        weigh[7 * f : 7 * f + 8, f] = WEIGHTS
        pick[7 * f : 7 * f + 7, f] = 1.0
        ends[7 * f + 7, f] = 1.0
    unit = np.eye(cap_x)
    widen = np.concatenate([np.kron(unit, weigh), np.kron(unit, pick), np.kron(unit, ends)], axis=0)
    widen = np.pad(widen, ((0, 0), (0, LANES - widen.shape[1])))
    factor = np.zeros((ROWS + 8, LANES))
    factor[: 7 * cap_y] = STIFF[np.arange(7 * cap_y) % 7, np.arange(7 * cap_y) % 7][:, None]
    factor[ROWS:, : 7 * layers] = STIFF[np.arange(7 * layers) % 7, np.arange(7 * layers) % 7][None, :]
    parts = [half for part in vertical for half in (part[:, :LANES], part[:, LANES:])]
    parts += [*across]
    parts += [depth[:, k * LANES : (k + 1) * LANES] for k in range(3)] + [widen, factor]
    return np.concatenate([part.astype(np.float32) for part in parts], axis=0)


def plane(x):
    return pl.ds(pl.multiple_of(x * ROWS, ROWS), ROWS)


def total(values):
    return jnp.sum(values, axis=(0, 1), keepdims=True)


def iota(shape, dim):
    return lax.broadcasted_iota(jnp.int32, shape, dim)


def pieces(values):
    first = values.astype(jnp.bfloat16)
    rest = values - first.astype(jnp.float32)
    second = rest.astype(jnp.bfloat16)
    third = (rest - second.astype(jnp.float32)).astype(jnp.bfloat16)
    return [first, second, third]


def exact_dot(values, chosen):
    rows = values.shape[0]
    result = jnp.dot(
        jnp.concatenate(pieces(values), axis=0), chosen, preferred_element_type=jnp.float32
    )
    return result[0:rows] + result[rows : 2 * rows] + result[2 * rows : 3 * rows]


def kernel(
    nx, ny, cap_x, cap_y, layers, bx, by,
    wx_ref, wy_ref, load_any, diff_any, kappa_any, factor_any,
    table_any,
    solution_ref, residual_ref,
    load_ref, diff_ref, kappa_ref, table_ref, vertical_ref, across_ref,
    f_z, f_im, f_w, f_d, f_r, f_sol, f_inv, f_share, f_mass, f_ya, f_yb, f_za, f_zb,
    e_px, e_big, e_ya, e_yb, squares, sq_kappa,
    rows_x, gather_map, spread_map,
    halo_sx, halo_sy, halo_sc, halo_rx, halo_ry, halo_rc,
    grid_s, grid_r, chunk_s, chunk_r, back_s, back_r, last_s, last_r, end_s, end_r,
    in_sem, own_sem, x_send, x_recv, ring_send, ring_recv,
    h_send, h_recv, r_send, r_recv, l_send, l_recv,
):
    p, q = lax.axis_index("gx"), lax.axis_index("gy")
    wx, wy = wx_ref[0], wy_ref[0]
    groups = chunk_s.shape[1] - 1
    width = groups * LANES
    end_x, end_y = 7 * wx, 7 * wy
    near, far = bx * by, (nx // bx) * (ny // by)
    ax, ay = nx // bx, ny // by
    bi, bj, ai, aj = lax.rem(p, bx), lax.rem(q, by), p // bx, q // by
    mine, block_id = bi * by + bj, ai * ay + aj

    def beside(dx, dy):
        return (lax.rem(p + dx + nx, nx), lax.rem(q + dy + ny, ny))

    def in_block(index):
        return (ai * bx + index // by, aj * by + lax.rem(index, by))

    def across(index):
        return (index // ay * bx + bi, lax.rem(index, ay) * by + bj)

    barrier = pltpu.get_barrier_semaphore()

    def greet(device):
        pl.semaphore_signal(barrier, inc=1, device_id=device, device_id_type=MESH)

    def greet_near(o, _):
        greet(in_block(lax.rem(mine + o, near)))
        return 0

    def greet_far(o, _):
        greet(across(lax.rem(block_id + o, far)))
        return 0

    lax.fori_loop(1, near, greet_near, 0)
    lax.fori_loop(1, far, greet_far, 0)
    for dx, dy in DIRECTIONS:
        greet(beside(dx, dy))

    arrivals = []
    for i, (source, target) in enumerate((
        (diff_any, diff_ref), (kappa_any, kappa_ref), (table_any, table_ref), (load_any, load_ref),
    )):
        copy = pltpu.make_async_copy(source, target, in_sem.at[i])
        copy.start()
        arrivals.append(copy)

    def remote(source, target, send, recv, device):
        return pltpu.make_async_remote_copy(
            src_ref=source,
            dst_ref=target,
            send_sem=send,
            recv_sem=recv,
            device_id=device,
            device_id_type=MESH,
        )

    def columns(index):
        return pl.ds(pl.multiple_of(index * width, LANES), width)

    def rows_of(j):
        return pl.ds(pl.multiple_of((j + 1) * 16, 16), 16)

    own_rows = pltpu.make_async_copy(
        factor_any.at[:, columns(mine)], rows_x.at[bi + 1, rows_of(bj), :], own_sem.at[0]
    )
    own_rows.start()

    def flag(condition):
        return jnp.where(condition, 1.0, 0.0).astype(jnp.float32)

    has_left, has_right = flag(p > 0), flag(p < nx - 1)
    has_below, has_above = flag(q > 0), flag(q < ny - 1)

    pl.semaphore_wait(barrier, near + far - 2 + len(DIRECTIONS))

    def scatter_copy(o):
        peer = lax.rem(mine + o, near)
        return remote(
            factor_any.at[:, columns(peer)],
            rows_x.at[bi + 1, rows_of(bj), :],
            x_send.at[o],
            x_recv.at[o],
            in_block(peer),
        )

    def scatter(o, _):
        scatter_copy(o).start()
        return 0

    lax.fori_loop(1, near, scatter, 0)

    squares[...] = jnp.zeros_like(squares)
    sq_kappa[...] = jnp.zeros_like(sq_kappa)
    for copy in arrivals[0:3]:
        copy.wait()
    inside = iota((cap_y, layers), 0) < wy
    tall = cap_x * ROWS
    base = 4 * LANES
    for g in range(2):
        lanes = slice(g * LANES, (g + 1) * LANES)
        high = table_ref[g * LANES : (g + 1) * LANES, :].astype(jnp.bfloat16)
        low = table_ref[(g + 2) * LANES : (g + 3) * LANES, :].astype(jnp.bfloat16)
        for k, part in enumerate((high, high, low)):
            vertical_ref[k * LANES : (k + 1) * LANES, lanes] = part
    high = table_ref[base : base + 2 * LANES, :].astype(jnp.bfloat16)
    low = table_ref[base + 2 * LANES : base + 4 * LANES, :].astype(jnp.bfloat16)
    for k, part in enumerate((high, high, low)):
        across_ref[:, k * LANES : (k + 1) * LANES] = part
    base = 8 * LANES
    depth_table = jnp.concatenate(
        [table_ref[base + k * LANES : base + (k + 1) * LANES, :] for k in range(3)], axis=1
    )
    base = 11 * LANES
    widen = table_ref[base : base + 3 * tall, :]
    base = base + 3 * tall
    for e in range(cap_x):
        keep = inside & (e < wx)
        squares[8 * e : 8 * e + cap_y, 0:layers] = jnp.where(keep, diff_ref[e], 0.0)
        sq_kappa[8 * e : 8 * e + cap_y, 0:layers] = jnp.where(keep, kappa_ref[e], 0.0)
    deep = jnp.dot(squares[...], depth_table, precision=HIGHEST, preferred_element_type=jnp.float32)
    deep_kappa = jnp.dot(
        sq_kappa[...], depth_table[:, 0:LANES], precision=HIGHEST, preferred_element_type=jnp.float32
    )
    big = jnp.dot(
        widen[0:tall, :],
        jnp.concatenate([deep, deep_kappa], axis=1),
        precision=HIGHEST,
        preferred_element_type=jnp.float32,
    )
    both = jnp.dot(
        widen[tall : 3 * tall, :],
        deep[:, 0:LANES],
        precision=HIGHEST,
        preferred_element_type=jnp.float32,
    )
    zero_plane = jnp.zeros((ROWS, LANES), jnp.float32)
    for ref in (e_px, e_ya, e_yb):
        ref[0:ROWS, :] = zero_plane
        ref[tall + ROWS : tall + 2 * ROWS, :] = zero_plane
    for place in (0, tall + ROWS):
        e_big[place : place + ROWS, :] = jnp.zeros((ROWS, 3 * LANES), jnp.float32)
    e_px[ROWS : ROWS + tall, :] = big[:, 0:LANES]
    e_big[ROWS : ROWS + tall, :] = big[:, LANES : 4 * LANES]
    e_ya[ROWS : ROWS + tall, :] = both[0:tall]
    e_yb[ROWS : ROWS + tall, :] = both[tall : 2 * tall]

    fields = (f_z, f_im, f_r, f_inv, f_mass, f_ya, f_yb, f_za, f_zb)
    for ref in fields:
        for x in range(7 * cap_x, PLANES):
            ref[x * ROWS : (x + 1) * ROWS, :] = zero_plane

    sources = (
        (f_za, e_big, 0), (f_zb, e_big, 1), (f_mass, e_big, 2), (f_ya, e_ya, 0), (f_yb, e_yb, 0),
    )
    row_factor = table_ref[base : base + ROWS, :]
    depth_factor = table_ref[base + ROWS : base + ROWS + 1, :]
    corner = float(STIFF[7, 7])

    def fill_plane(x, e, b):
        values = []
        for target, source, lane in sources:
            lanes = slice(lane * LANES, (lane + 1) * LANES)
            value = float(WEIGHTS[b]) * source[plane(e + 1), lanes]
            if b == 0:
                value = value + float(WEIGHTS[7]) * source[plane(e), lanes]
            target[plane(x), :] = value
            values.append(value)
        za, zb, mass, ya, yb = values
        diagonal = mass + ya * row_factor + yb * corner + za * depth_factor + zb * corner
        diagonal = diagonal + float(STIFF[b, b]) * e_px[plane(e + 1), :]
        if b == 0:
            diagonal = diagonal + float(STIFF[7, 7]) * e_px[plane(e), :]
        f_inv[plane(x), :] = diagonal

    def fill(e, _):
        for b in range(7):
            fill_plane(7 * e + b, e, b)
        return 0

    lax.fori_loop(0, cap_x, fill, 0)
    fill_plane(7 * cap_x, cap_x, 0)

    slots_x, slots_y = load_ref.shape[0], load_ref.shape[1]
    row = iota((slots_y, LANES), 0)
    real = iota((slots_y, LANES), 1) <= 7 * layers
    f_r[...] = jnp.zeros_like(f_r)
    arrivals[3].wait()

    def take(x, _):
        value = jnp.where(x < end_x, load_ref[x], jnp.where(x == end_x, load_ref[slots_x - 1], 0.0))
        last = value[slots_y - 1 : slots_y, :]
        value = jnp.where(row < end_y, value, jnp.where(row == end_y, last, 0.0))
        f_r[pl.ds(pl.multiple_of(x * ROWS, ROWS), slots_y), :] = jnp.where(real, value, 0.0)
        return 0

    lax.fori_loop(0, slots_x, take, 0)

    def high_plane(ref):
        value = jnp.zeros((ROWS, LANES), jnp.float32)
        for j in range(1, cap_x + 1):
            value = value + jnp.where(wx == j, ref[7 * j * ROWS : (7 * j + 1) * ROWS, :], 0.0)
        return value

    def side(j):
        return pl.ds(7 * j, PLANES, stride=ROWS)

    def high_row(plane_value):
        value = jnp.zeros((1, LANES), jnp.float32)
        for j in range(1, cap_y + 1):
            value = value + jnp.where(wy == j, plane_value[7 * j : 7 * j + 1, :], 0.0)
        return value

    def halo_copies(h):
        copies = []
        for k, (dx, dy) in enumerate(DIRECTIONS):
            if dy == 0:
                slot = (h, 0 if dx > 0 else 1)
                source, target = halo_sx.at[slot], halo_rx.at[slot]
            elif dx == 0:
                slot = (h, 0 if dy > 0 else 1)
                source, target = halo_sy.at[slot], halo_ry.at[slot]
            else:
                source, target = halo_sc.at[h, k - 4], halo_rc.at[h, k - 4]
            copies.append(remote(source, target, h_send.at[h, k], h_recv.at[h, k], beside(dx, dy)))
        return copies

    def halo_start(h, ref):
        low, high = ref[0:ROWS, :], high_plane(ref)
        halo_sx[h, 0] = high
        halo_sx[h, 1] = low
        above = jnp.zeros((PLANES, LANES), jnp.float32)
        for j in range(1, cap_y + 1):
            above = above + jnp.where(wy == j, ref[side(j), :], 0.0)
        halo_sy[h, 0] = above
        halo_sy[h, 1] = ref[side(0), :]
        rows = (high_row(high), high[0:1, :], high_row(low), low[0:1, :])
        for k, value in enumerate(rows):
            halo_sc[h, k] = jnp.broadcast_to(value, (8, LANES))
        copies = halo_copies(h)
        for copy in copies:
            copy.start()
        return copies

    place = iota((PLANES, LANES), 0)

    def halo_finish(h, ref, copies):
        for copy in copies:
            copy.wait()
        ref[0:ROWS, :] = ref[0:ROWS, :] + has_left * halo_rx[h, 0]
        from_right = has_right * halo_rx[h, 1]
        for j in range(1, cap_x + 1):
            rows = slice(7 * j * ROWS, (7 * j + 1) * ROWS)
            ref[rows, :] = ref[rows, :] + jnp.where(wx == j, from_right, 0.0)

        def line(side_value, first, second):
            side_value = side_value + jnp.where(place == 0, has_left * first[0:1, :], 0.0)
            return side_value + jnp.where(place == end_x, has_right * second[0:1, :], 0.0)

        below = has_below * line(halo_ry[h, 0], halo_rc[h, 0], halo_rc[h, 2])
        above = has_above * line(halo_ry[h, 1], halo_rc[h, 1], halo_rc[h, 3])
        ref[side(0), :] = ref[side(0), :] + below
        for j in range(1, cap_y + 1):
            ref[side(j), :] = ref[side(j), :] + jnp.where(wy == j, above, 0.0)

    deep_node, deep_lane = iota((LANES, LANES), 0), iota((LANES, LANES), 1)
    for dy in (-1, 0, 1):
        part = slice((dy + 1) * LANES, (dy + 2) * LANES)
        start = (bj + 1 + dy) * 16
        gather_map[part, :] = flag(deep_lane == start + deep_node // 8).astype(jnp.bfloat16)
        spread_map[:, part] = flag(deep_node == start + deep_lane // 8).astype(jnp.bfloat16)
    grid_row = iota((8, LANES), 0)
    row32 = iota((ROWS, LANES), 0)
    chunk = 4 * ROWS
    chunks = (7 * cap_x + 4) // 4

    def coarse_sums(ref):
        def add(i, value):
            return value + jnp.sum(
                ref[pl.ds(pl.multiple_of(i * chunk, chunk), chunk), :].reshape(4, ROWS, LANES), axis=0
            )

        middle = lax.fori_loop(0, chunks, add, zero_plane, unroll=True)
        low, high = 0.5 * has_left * ref[0:ROWS, :], 0.5 * has_right * high_plane(ref)
        sums = [jnp.zeros((8, LANES), jnp.float32)] * 3
        for dx, value in ((-1, low), (0, middle - low - high), (1, high)):
            below = 0.5 * has_below * value[0:1, :]
            above = 0.5 * has_above * high_row(value)
            centre = jnp.sum(value, axis=0, keepdims=True) - below - above
            for k, profile in enumerate((below, centre, above)):
                sums[k] = sums[k] + jnp.where(grid_row == bi + 1 + dx, profile, 0.0)
        return exact_dot(jnp.concatenate(sums, axis=1), gather_map[...])

    def wait_in(buffer, count, send, recv):
        part = buffer.at[pl.ds(0, count)]
        remote(part, part, send, recv, beside(1, 0)).wait_recv()

    def wait_out(buffer, count, send, recv):
        part = buffer.at[pl.ds(0, count)]
        remote(part, part, send, recv, beside(1, 0)).wait_send()

    def exchange_start(source, target, count, me, device, send, recv):
        def go(o, _):
            remote(source, target.at[me], send, recv, device(lax.rem(me + o, count))).start()
            return 0

        lax.fori_loop(1, count, go, 0)
        target[me] = source[...]

    def reduce_start(a, ref):
        grid_s[a] = coarse_sums(ref)
        exchange_start(
            grid_s.at[a], grid_r.at[a], near, mine, in_block, r_send.at[a, 0], r_recv.at[a, 0]
        )

    lane = iota((1, LANES), 1)

    def scalar_row(values):
        result = jnp.zeros((1, LANES), jnp.float32)
        for i, value in enumerate(values):
            result = jnp.where(lane == i, value, result)
        return result

    def pick(values, i):
        return total(jnp.where(lane == i, values, 0.0))

    grid_rows, grid_lanes = bx + 2, (by + 2) * 16

    def reduce_middle(a, scalars):
        wait_in(grid_r.at[a], near - 1, r_send.at[a, 0], r_recv.at[a, 0])
        turned = jnp.sum(grid_r[a], axis=0).T
        value = jnp.zeros((8, width), jnp.float32)
        for i in range(grid_rows):
            product = rows_x[i] * turned[0:grid_lanes, i : i + 1]
            value = value + jnp.sum(product.reshape(grid_lanes // 8, 8, width), axis=0)
        value = jnp.sum(value, axis=0, keepdims=True)
        for g in range(groups):
            chunk_s[a, g : g + 1, :] = value[:, g * LANES : (g + 1) * LANES]
        chunk_s[a, groups : groups + 1, :] = scalar_row(scalars)
        exchange_start(
            chunk_s.at[a], chunk_r.at[a], far, block_id, across, r_send.at[a, 1], r_recv.at[a, 1]
        )

    def reduce_finish(a, extra):
        wait_in(chunk_r.at[a], far - 1, r_send.at[a, 1], r_recv.at[a, 1])
        sums = jnp.sum(chunk_r[a], axis=0)
        through = sums[0:groups, :]
        turned = jnp.zeros((grid_lanes, LANES), jnp.float32)
        wide_lane = iota((grid_lanes, LANES), 1)
        for i in range(grid_rows):
            product = rows_x[i, :, 0:LANES] * through[0:1, :]
            for g in range(1, groups):
                product = product + rows_x[i, :, g * LANES : (g + 1) * LANES] * through[g : g + 1, :]
            turned = jnp.where(wide_lane == i, jnp.sum(product, axis=1, keepdims=True), turned)
        turned = jnp.concatenate(
            [turned, jnp.zeros((LANES - grid_lanes, LANES), jnp.float32)], axis=0
        )
        scalars = sums[groups : groups + 1, :]
        if extra is not None:
            scalars = jnp.where(lane == 8, extra, scalars)
        back_s[a] = jnp.where(grid_row == 7, scalars, turned.T[0:8, :])
        exchange_start(
            back_s.at[a], back_r.at[a], near, mine, in_block, r_send.at[a, 2], r_recv.at[a, 2]
        )
        wait_in(back_r.at[a], near - 1, r_send.at[a, 2], r_recv.at[a, 2])
        grid = jnp.sum(back_r[a], axis=0)
        wait_out(grid_r.at[a], near - 1, r_send.at[a, 0], r_recv.at[a, 0])
        wait_out(chunk_r.at[a], far - 1, r_send.at[a, 1], r_recv.at[a, 1])
        wait_out(back_r.at[a], near - 1, r_send.at[a, 2], r_recv.at[a, 2])
        return grid, grid[7:8, :], through

    def coarse_planes(grid):
        deep_values = exact_dot(grid, spread_map[...])

        def spread(dx):
            line = jnp.sum(jnp.where(iota((8, 3 * LANES), 0) == bi + 1 + dx, deep_values, 0.0), axis=0, keepdims=True)
            below, centre, above = (line[:, k * LANES : (k + 1) * LANES] for k in range(3))
            value = jnp.where(row32 == 0, centre + 0.5 * has_below * (below - centre), centre)
            return jnp.where(row32 == end_y, value + 0.5 * has_above * (above - centre), value)

        middle = spread(0)
        first = middle + 0.5 * has_left * (spread(-1) - middle)
        second = middle + 0.5 * has_right * (spread(1) - middle)
        return first, middle, second

    def coarse_at(x, planes):
        first, middle, second = planes
        return jnp.where(x == 0, first, jnp.where(x == end_x, second, middle))

    def apply_operator():
        def along_x(e, carried):
            values = [f_z[plane(7 * e + c), :] for c in range(8)]
            sums = [values[c] + values[7 - c] for c in range(4)]
            gaps = [values[c] - values[7 - c] for c in range(4)]
            scale = e_px[plane(e + 1), :]
            results = [None] * 8
            for b in range(4):
                even = sum(float(0.5 * (STIFF[b, c] + STIFF[b, 7 - c])) * sums[c] for c in range(4))
                odd = sum(float(0.5 * (STIFF[b, c] - STIFF[b, 7 - c])) * gaps[c] for c in range(4))
                results[b] = scale * (even + odd)
                results[7 - b] = scale * (even - odd)
            f_im[plane(7 * e), :] = carried + results[0]
            for b in range(1, 7):
                f_im[plane(7 * e + b), :] = results[b]
            return results[7]

        carried = lax.fori_loop(0, cap_x, along_x, zero_plane, unroll=True)
        f_im[plane(7 * cap_x), :] = carried

        def along_rest(i, product):
            rows = pl.ds(pl.multiple_of(i * chunk, chunk), chunk)
            value = f_z[rows, :]
            high = value.astype(jnp.bfloat16)
            low = (value - high.astype(jnp.float32)).astype(jnp.bfloat16)
            deep = jnp.dot(
                jnp.concatenate([high, low, high], axis=1),
                vertical_ref[...],
                preferred_element_type=jnp.float32,
            )
            wide = jnp.dot(
                across_ref[...],
                jnp.concatenate([high, low, high], axis=0),
                preferred_element_type=jnp.float32,
            )
            image = f_im[rows, :] + f_mass[rows, :] * value
            image = image + f_ya[rows, :] * wide[0:chunk] + f_yb[rows, :] * wide[chunk:]
            image = image + f_za[rows, :] * deep[:, 0:LANES] + f_zb[rows, :] * deep[:, LANES:]
            f_im[rows, :] = image
            return product + jnp.sum((value * image).reshape(chunk // 8, 8, LANES), axis=0)

        product = lax.fori_loop(0, chunks, along_rest, jnp.zeros((8, LANES), jnp.float32), unroll=True)
        return total(product)

    reduce_start(0, f_r)
    load_copies = halo_start(0, f_r)
    diagonal_copies = halo_start(1, f_inv)

    own_rows.wait()

    def scatter_wait(o, _):
        scatter_copy(o).wait()
        return 0

    lax.fori_loop(1, near, scatter_wait, 0)
    spans = {1: (slice(bx, bx + 1), slice(0, 1)), -1: (slice(1, 2), slice(bx + 1, bx + 2))}
    spans[0] = (slice(1, bx + 1), slice(1, bx + 1))
    across_spans = {1: (by, 0, 1), -1: (1, by + 1, 1), 0: (1, 1, by)}
    ring = []
    for k, (dx, dy) in enumerate(DIRECTIONS):
        (source_x, target_x), (source_y, target_y, count) = spans[dx], across_spans[dy]
        copy = remote(
            rows_x.at[source_x, pl.ds(source_y * 16, count * 16), :],
            rows_x.at[target_x, pl.ds(target_y * 16, count * 16), :],
            ring_send.at[k],
            ring_recv.at[k],
            beside(dx * bx, dy * by),
        )
        copy.start()
        ring.append(copy)

    halo_finish(0, f_r, load_copies)
    halo_finish(1, f_inv, diagonal_copies)
    share_low = jnp.where(row32 == 0, 1.0 - 0.5 * has_below, 1.0)
    share_row = jnp.where(row32 == end_y, 1.0 - 0.5 * has_above, share_low)

    def share_x(x):
        low = jnp.where(x == 0, 1.0 - 0.5 * has_left, 1.0)
        return jnp.where(x == end_x, 1.0 - 0.5 * has_right, low)

    def invert(x, value):
        diagonal = f_inv[plane(x), :]
        inverse = jnp.where(diagonal > 0.0, 1.0 / jnp.where(diagonal > 0.0, diagonal, 1.0), 0.0)
        f_inv[plane(x), :] = inverse
        share = jnp.where(diagonal > 0.0, share_row * share_x(x), 0.0)
        f_share[plane(x), :] = share
        resid = f_r[plane(x), :]
        f_sol[plane(x), :] = zero_plane
        f_w[plane(x), :] = zero_plane
        f_d[plane(x), :] = zero_plane
        return value + share * inverse * resid * resid

    planes = 7 * cap_x + 1
    jacobi = total(lax.fori_loop(0, planes, invert, zero_plane))
    for copy in ring:
        copy.wait()
    reduce_middle(0, [])
    grid, _, through = reduce_finish(0, None)
    coarse = coarse_planes(grid)

    def begin(x, _):
        inverse = f_inv[plane(x), :]
        value = jnp.where(inverse > 0.0, coarse_at(x, coarse), 0.0)
        f_z[plane(x), :] = inverse * f_r[plane(x), :] + value
        return 0

    lax.fori_loop(0, planes, begin, 0)

    cross = jnp.zeros((1, 1), jnp.float32)
    beta, rho, curvature = cross, None, cross
    through_w, grid_w = jnp.zeros_like(through), jnp.zeros_like(grid)

    def scalars_of(values, squared):
        rho_now = pick(values, 2) + squared
        beta_now = jnp.zeros((1, 1), jnp.float32) if rho is None else rho_now / rho
        bent = pick(values, 0) + 2.0 * beta_now * pick(values, 1) + beta_now * beta_now * curvature
        return rho_now, beta_now, bent

    for i in range(ITERS):
        own = apply_operator()
        squared = total(through * through)
        if i + 1 < ITERS:
            reduce_start(i + 1, f_im)
            image_copies = halo_start(2 + i, f_im)
            reduce_middle(i + 1, [own, cross, jacobi])
            halo_finish(2 + i, f_im, image_copies)
            grid_q, values, through_q = reduce_finish(i + 1, squared)
            rho, beta, curvature = scalars_of(values, pick(values, 8))
            step = rho / curvature
            grid_w = grid_q + beta * grid_w
            through_w = through_q + beta * through_w
            grid = grid - step * grid_w
            through = through - step * through_w
            coarse = coarse_planes(grid)

            def advance(x, sums):
                here = plane(x)
                old = f_z[here, :]
                direction = old + beta * f_d[here, :]
                image = f_im[here, :] + beta * f_w[here, :]
                f_d[here, :] = direction
                f_w[here, :] = image
                f_sol[here, :] = f_sol[here, :] + step * direction
                resid = f_r[here, :] - step * image
                f_r[here, :] = resid
                scaled = f_inv[here, :] * resid
                share = f_share[here, :]
                value = scaled + jnp.where(share > 0.0, coarse_at(x, coarse), 0.0)
                f_z[here, :] = value
                return sums[0] + share * scaled * resid, sums[1] + share * value * image

            jacobi, cross = lax.fori_loop(
                0, planes, advance, (zero_plane, zero_plane), unroll=True
            )
            jacobi, cross = total(jacobi), total(cross)
        else:
            last_s[...] = scalar_row([own, cross, jacobi])
            exchange_start(last_s, last_r, far, block_id, across, l_send.at[0], l_recv.at[0])
            image_copies = halo_start(2 + i, f_im)
            halo_finish(2 + i, f_im, image_copies)
            wait_in(last_r, far - 1, l_send.at[0], l_recv.at[0])
            end_s[...] = jnp.where(lane == 8, squared, jnp.sum(last_r[...], axis=0))
            exchange_start(end_s, end_r, near, mine, in_block, l_send.at[1], l_recv.at[1])
            wait_in(end_r, near - 1, l_send.at[1], l_recv.at[1])
            values = jnp.sum(end_r[...], axis=0)
            rho, beta, curvature = scalars_of(values, pick(values, 8))
            step = rho / curvature
            wait_out(last_r, far - 1, l_send.at[0], l_recv.at[0])
            wait_out(end_r, near - 1, l_send.at[1], l_recv.at[1])

    def put(target, x, value):
        last = high_row(value)
        rows = value[0:slots_y, :]
        rows = jnp.where(row < end_y, rows, jnp.where(row == slots_y - 1, last, 0.0))
        target[x] = rows

    def finish(x, _):
        here = plane(x)
        found = f_sol[here, :] + step * (f_z[here, :] + beta * f_d[here, :])
        resid = f_r[here, :] - step * (f_im[here, :] + beta * f_w[here, :])
        f_sol[here, :] = found
        f_r[here, :] = resid
        put(solution_ref, x, jnp.where(x < end_x, found, 0.0))
        put(residual_ref, x, jnp.where(x < end_x, resid, 0.0))
        return 0

    lax.fori_loop(0, planes, finish, 0)
    put(solution_ref, slots_x - 1, high_plane(f_sol))
    put(residual_ref, slots_x - 1, high_plane(f_r))


def body(nx, ny, right_side, diffusion, kappa, widths_x, widths_y, factor):
    cap_x, cap_y, layers = diffusion.shape
    bx, by = BLOCK, BLOCK
    near, far = bx * by, (nx // bx) * (ny // by)
    groups = factor.shape[1] // (near * LANES)
    f32, bf16 = jnp.float32, jnp.bfloat16
    smem = pl.BlockSpec(memory_space=pltpu.SMEM)
    vmem = pl.BlockSpec(memory_space=pltpu.VMEM)
    hbm = pl.BlockSpec(memory_space=pltpu.HBM)
    tall = cap_x * ROWS
    dma = pltpu.SemaphoreType.DMA
    table = jnp.asarray(tables(cap_x, cap_y, layers))

    def room(*shape, dtype=f32):
        return pltpu.VMEM(shape, dtype)

    scratch = [room(*array.shape) for array in (right_side, diffusion, kappa, table)]
    scratch += [room(3 * LANES, 2 * LANES, dtype=bf16), room(2 * LANES, 3 * LANES, dtype=bf16)]
    scratch += [room(PLANES * ROWS, LANES)] * 13
    scratch += [
        room(tall + 2 * ROWS, LANES),
        room(tall + 2 * ROWS, 3 * LANES),
        room(tall + 2 * ROWS, LANES),
        room(tall + 2 * ROWS, LANES),
        room(LANES, LANES),
        room(LANES, LANES),
        room(bx + 2, (by + 2) * 16, groups * LANES),
        room(3 * LANES, LANES, dtype=bf16),
        room(LANES, 3 * LANES, dtype=bf16),
    ]
    halos = 2 + ITERS
    for _ in range(2):
        scratch += [
            room(halos, 2, ROWS, LANES),
            room(halos, 2, PLANES, LANES),
            room(halos, 4, 8, LANES),
        ]
    scratch += [
        room(ITERS, 8, LANES),
        room(ITERS, near, 8, LANES),
        room(ITERS, groups + 1, LANES),
        room(ITERS, far, groups + 1, LANES),
        room(ITERS, 8, LANES),
        room(ITERS, near, 8, LANES),
        room(1, LANES),
        room(far, 1, LANES),
        room(1, LANES),
        room(near, 1, LANES),
        dma((4,)), dma((1,)), dma((near,)), dma((near,)), dma((8,)), dma((8,)),
        dma((halos, 8)), dma((halos, 8)), dma((ITERS, 3)), dma((ITERS, 3)), dma((2,)), dma((2,)),
    ]
    shape = jax.ShapeDtypeStruct(right_side.shape, f32)
    return pl.pallas_call(
        functools.partial(kernel, nx, ny, cap_x, cap_y, layers, bx, by),
        out_shape=(shape, shape),
        in_specs=[smem, smem] + [hbm] * 5,
        out_specs=(vmem, vmem),
        scratch_shapes=scratch,
        compiler_params=pltpu.CompilerParams(
            collective_id=0, has_side_effects=True, vmem_limit_bytes=60 * 1024 * 1024
        ),
    )(widths_x, widths_y, right_side, diffusion, kappa, factor, table)


def solution(mesh):
    nx, ny = mesh.shape["gx"], mesh.shape["gy"]
    in_specs = (
        P("gx", "gy", None),
        P("gx", "gy", None),
        P("gx", "gy", None),
        P("gx"),
        P("gy"),
        P(("gx", "gy"), None),
    )
    out_specs = (P("gx", "gy", None), P("gx", "gy", None))
    return jax.shard_map(
        functools.partial(body, nx, ny),
        mesh=mesh,
        in_specs=in_specs,
        out_specs=out_specs,
        check_vma=False,
    )
```

```python
import functools

import jax
import jax.numpy as jnp
import ml_dtypes
import numpy as np
from jax import lax
from jax.experimental import pallas as pl
from jax.experimental.pallas import tpu as pltpu
from jax.sharding import PartitionSpec as P

ITERS = 3
HIGHEST = lax.Precision.HIGHEST
MESH = pl.DeviceIdType.MESH
LANES = 128
ROWS = 32
PLANES = 48
BLOCK = 4
DIRECTIONS = [(1, 0), (-1, 0), (0, 1), (0, -1), (1, 1), (1, -1), (-1, 1), (-1, -1)]


def gll_weights():
    return np.array(
        [
            1.0 / 28.0,
            0.2107042271435061,
            0.3411226924835044,
            0.4124587946587038,
            0.4124587946587038,
            0.3411226924835044,
            0.2107042271435061,
            1.0 / 28.0,
        ]
    )


def gll_derivative():
    points = np.array(
        [
            -1.0,
            -0.8717401485096066,
            -0.5917001814331423,
            -0.2092992179024789,
            0.2092992179024789,
            0.5917001814331423,
            0.8717401485096066,
            1.0,
        ]
    )
    identity = np.eye(8) > 0
    spacing = np.where(identity, 1.0, points[:, None] - points[None, :])
    barycentric = 1.0 / np.prod(spacing, axis=1)
    matrix = np.where(identity, 0.0, barycentric[None, :] / barycentric[:, None] / spacing)
    return np.where(identity, -np.sum(matrix, axis=1)[:, None], matrix)


WEIGHTS = gll_weights()
STIFF = gll_derivative().T @ np.diag(WEIGHTS) @ gll_derivative()


def split(matrix):
    high = matrix.astype(ml_dtypes.bfloat16)
    low = (matrix - high.astype(np.float64)).astype(ml_dtypes.bfloat16)
    return high, low


def band(cells, size):
    first, second = np.zeros((size, size)), np.zeros((size, size))
    for e in range(cells):
        for b in range(7):
            first[7 * e + b, 7 * e : 7 * e + 8] = STIFF[b]
        second[7 * e + 7, 7 * e : 7 * e + 8] = STIFF[7]
    return first, second


def tables(cap_x, cap_y, layers):
    first, second = band(layers, LANES)
    vertical = split(np.concatenate([first, second], axis=0).T)
    first, second = band(cap_y, ROWS)
    stacked = np.concatenate([np.kron(np.eye(4), first), np.kron(np.eye(4), second)], axis=0)
    across = split(stacked)
    depth = np.zeros((LANES, 3 * LANES))
    for h in range(layers):
        depth[h, 7 * h : 7 * h + 8] = WEIGHTS
        depth[h, LANES + 7 * h : LANES + 7 * h + 7] = 1.0
        depth[h, 2 * LANES + 7 * h + 7] = 1.0
    weigh, pick, ends = np.zeros((ROWS, 8)), np.zeros((ROWS, 8)), np.zeros((ROWS, 8))
    for f in range(cap_y):
        weigh[7 * f : 7 * f + 8, f] = WEIGHTS
        pick[7 * f : 7 * f + 7, f] = 1.0
        ends[7 * f + 7, f] = 1.0
    unit = np.eye(cap_x)
    widen = np.concatenate([np.kron(unit, weigh), np.kron(unit, pick), np.kron(unit, ends)], axis=0)
    widen = np.pad(widen, ((0, 0), (0, LANES - widen.shape[1])))
    factor = np.zeros((ROWS + 8, LANES))
    factor[: 7 * cap_y] = STIFF[np.arange(7 * cap_y) % 7, np.arange(7 * cap_y) % 7][:, None]
    factor[ROWS:, : 7 * layers] = STIFF[np.arange(7 * layers) % 7, np.arange(7 * layers) % 7][None, :]
    parts = [half for part in vertical for half in (part[:, :LANES], part[:, LANES:])]
    parts += [*across]
    parts += [depth[:, k * LANES : (k + 1) * LANES] for k in range(3)] + [widen, factor]
    return np.concatenate([part.astype(np.float32) for part in parts], axis=0)


def plane(x):
    return pl.ds(pl.multiple_of(x * ROWS, ROWS), ROWS)


def total(values):
    return jnp.sum(values, axis=(0, 1), keepdims=True)


def iota(shape, dim):
    return lax.broadcasted_iota(jnp.int32, shape, dim)


def pieces(values):
    first = values.astype(jnp.bfloat16)
    rest = values - first.astype(jnp.float32)
    second = rest.astype(jnp.bfloat16)
    third = (rest - second.astype(jnp.float32)).astype(jnp.bfloat16)
    return [first, second, third]


def exact_dot(values, chosen):
    rows = values.shape[0]
    result = jnp.dot(
        jnp.concatenate(pieces(values), axis=0), chosen, preferred_element_type=jnp.float32
    )
    return result[0:rows] + result[rows : 2 * rows] + result[2 * rows : 3 * rows]


def kernel(
    nx, ny, cap_x, cap_y, layers, bx, by,
    wx_ref, wy_ref, load_any, diff_any, kappa_any, factor_any,
    table_any,
    solution_ref, residual_ref,
    load_ref, diff_ref, kappa_ref, table_ref, vertical_ref, across_ref,
    f_z, f_im, f_w, f_d, f_r, f_sol, f_inv, f_share, f_mass, f_ya, f_yb, f_za, f_zb,
    e_px, e_big, e_ya, e_yb, squares, sq_kappa,
    rows_x, gather_map, spread_map,
    halo_sx, halo_sy, halo_sc, halo_rx, halo_ry, halo_rc,
    grid_s, grid_r, chunk_s, chunk_r, back_s, back_r, last_s, last_r, end_s, end_r,
    in_sem, own_sem, x_send, x_recv, ring_send, ring_recv,
    h_send, h_recv, r_send, r_recv, l_send, l_recv,
):
    p, q = lax.axis_index("gx"), lax.axis_index("gy")
    wx, wy = wx_ref[0], wy_ref[0]
    groups = chunk_s.shape[1] - 1
    width = groups * LANES
    end_x, end_y = 7 * wx, 7 * wy
    near, far = bx * by, (nx // bx) * (ny // by)
    ax, ay = nx // bx, ny // by
    bi, bj, ai, aj = lax.rem(p, bx), lax.rem(q, by), p // bx, q // by
    mine, block_id = bi * by + bj, ai * ay + aj

    def beside(dx, dy):
        return (lax.rem(p + dx + nx, nx), lax.rem(q + dy + ny, ny))

    def in_block(index):
        return (ai * bx + index // by, aj * by + lax.rem(index, by))

    def across(index):
        return (index // ay * bx + bi, lax.rem(index, ay) * by + bj)

    barrier = pltpu.get_barrier_semaphore()

    def greet(device):
        pl.semaphore_signal(barrier, inc=1, device_id=device, device_id_type=MESH)

    def greet_near(o, _):
        greet(in_block(lax.rem(mine + o, near)))
        return 0

    def greet_far(o, _):
        greet(across(lax.rem(block_id + o, far)))
        return 0

    lax.fori_loop(1, near, greet_near, 0, unroll=True)
    lax.fori_loop(1, far, greet_far, 0, unroll=True)
    for dx, dy in DIRECTIONS:
        greet(beside(dx, dy))

    arrivals = []
    for i, (source, target) in enumerate((
        (diff_any, diff_ref), (kappa_any, kappa_ref), (table_any, table_ref), (load_any, load_ref),
    )):
        copy = pltpu.make_async_copy(source, target, in_sem.at[i])
        copy.start()
        arrivals.append(copy)

    def remote(source, target, send, recv, device):
        return pltpu.make_async_remote_copy(
            src_ref=source,
            dst_ref=target,
            send_sem=send,
            recv_sem=recv,
            device_id=device,
            device_id_type=MESH,
        )

    def columns(index):
        return pl.ds(pl.multiple_of(index * width, LANES), width)

    def rows_of(j):
        return pl.ds(pl.multiple_of((j + 1) * 16, 16), 16)

    own_rows = pltpu.make_async_copy(
        factor_any.at[:, columns(mine)], rows_x.at[bi + 1, rows_of(bj), :], own_sem.at[0]
    )
    own_rows.start()

    def flag(condition):
        return jnp.where(condition, 1.0, 0.0).astype(jnp.float32)

    has_left, has_right = flag(p > 0), flag(p < nx - 1)
    has_below, has_above = flag(q > 0), flag(q < ny - 1)

    def scatter_copy(o):
        peer = lax.rem(mine + o, near)
        return remote(
            factor_any.at[:, columns(peer)],
            rows_x.at[bi + 1, rows_of(bj), :],
            x_send.at[o],
            x_recv.at[o],
            in_block(peer),
        )

    def scatter(o, _):
        scatter_copy(o).start()
        return 0

    zero_plane = jnp.zeros((ROWS, LANES), jnp.float32)
    slots_x, slots_y = load_ref.shape[0], load_ref.shape[1]
    row = iota((slots_y, LANES), 0)
    real = iota((slots_y, LANES), 1) <= 7 * layers
    f_r[...] = jnp.zeros_like(f_r)
    arrivals[3].wait()

    def take(x, _):
        value = jnp.where(x < end_x, load_ref[x], jnp.where(x == end_x, load_ref[slots_x - 1], 0.0))
        last = value[slots_y - 1 : slots_y, :]
        value = jnp.where(row < end_y, value, jnp.where(row == end_y, last, 0.0))
        f_r[pl.ds(pl.multiple_of(x * ROWS, ROWS), slots_y), :] = jnp.where(real, value, 0.0)
        return 0

    lax.fori_loop(0, slots_x, take, 0)

    def high_plane(ref):
        value = jnp.zeros((ROWS, LANES), jnp.float32)
        for j in range(1, cap_x + 1):
            value = value + jnp.where(wx == j, ref[7 * j * ROWS : (7 * j + 1) * ROWS, :], 0.0)
        return value

    def side(j):
        return pl.ds(7 * j, PLANES, stride=ROWS)

    def high_row(plane_value):
        value = jnp.zeros((1, LANES), jnp.float32)
        for j in range(1, cap_y + 1):
            value = value + jnp.where(wy == j, plane_value[7 * j : 7 * j + 1, :], 0.0)
        return value

    def halo_copies(h):
        copies = []
        for k, (dx, dy) in enumerate(DIRECTIONS):
            if dy == 0:
                slot = (h, 0 if dx > 0 else 1)
                source, target = halo_sx.at[slot], halo_rx.at[slot]
            elif dx == 0:
                slot = (h, 0 if dy > 0 else 1)
                source, target = halo_sy.at[slot], halo_ry.at[slot]
            else:
                source, target = halo_sc.at[h, k - 4], halo_rc.at[h, k - 4]
            copies.append(remote(source, target, h_send.at[h, k], h_recv.at[h, k], beside(dx, dy)))
        return copies

    def halo_pack(h, ref):
        low, high = ref[0:ROWS, :], high_plane(ref)
        halo_sx[h, 0] = high
        halo_sx[h, 1] = low
        above = jnp.zeros((PLANES, LANES), jnp.float32)
        for j in range(1, cap_y + 1):
            above = above + jnp.where(wy == j, ref[side(j), :], 0.0)
        halo_sy[h, 0] = above
        halo_sy[h, 1] = ref[side(0), :]
        rows = (high_row(high), high[0:1, :], high_row(low), low[0:1, :])
        for k, value in enumerate(rows):
            halo_sc[h, k] = jnp.broadcast_to(value, (8, LANES))

    def halo_send(h):
        copies = halo_copies(h)
        for copy in copies:
            copy.start()
        return copies

    def halo_start(h, ref):
        halo_pack(h, ref)
        return halo_send(h)

    place = iota((PLANES, LANES), 0)

    def halo_finish(h, ref, copies):
        for copy in copies:
            copy.wait()
        ref[0:ROWS, :] = ref[0:ROWS, :] + has_left * halo_rx[h, 0]
        from_right = has_right * halo_rx[h, 1]
        for j in range(1, cap_x + 1):
            rows = slice(7 * j * ROWS, (7 * j + 1) * ROWS)
            ref[rows, :] = ref[rows, :] + jnp.where(wx == j, from_right, 0.0)

        def line(side_value, first, second):
            side_value = side_value + jnp.where(place == 0, has_left * first[0:1, :], 0.0)
            return side_value + jnp.where(place == end_x, has_right * second[0:1, :], 0.0)

        below = has_below * line(halo_ry[h, 0], halo_rc[h, 0], halo_rc[h, 2])
        above = has_above * line(halo_ry[h, 1], halo_rc[h, 1], halo_rc[h, 3])
        ref[side(0), :] = ref[side(0), :] + below
        for j in range(1, cap_y + 1):
            ref[side(j), :] = ref[side(j), :] + jnp.where(wy == j, above, 0.0)

    halo_pack(0, f_r)
    pl.semaphore_wait(barrier, near + far - 2 + len(DIRECTIONS))

    load_copies = halo_send(0)
    lax.fori_loop(1, near, scatter, 0, unroll=True)

    squares[...] = jnp.zeros_like(squares)
    sq_kappa[...] = jnp.zeros_like(sq_kappa)
    for copy in arrivals[0:3]:
        copy.wait()
    inside = iota((cap_y, layers), 0) < wy
    tall = cap_x * ROWS
    base = 4 * LANES
    for g in range(2):
        lanes = slice(g * LANES, (g + 1) * LANES)
        high = table_ref[g * LANES : (g + 1) * LANES, :].astype(jnp.bfloat16)
        low = table_ref[(g + 2) * LANES : (g + 3) * LANES, :].astype(jnp.bfloat16)
        for k, part in enumerate((high, high, low)):
            vertical_ref[k * LANES : (k + 1) * LANES, lanes] = part
    high = table_ref[base : base + 2 * LANES, :].astype(jnp.bfloat16)
    low = table_ref[base + 2 * LANES : base + 4 * LANES, :].astype(jnp.bfloat16)
    for k, part in enumerate((high, high, low)):
        across_ref[:, k * LANES : (k + 1) * LANES] = part
    base = 8 * LANES
    depth_table = jnp.concatenate(
        [table_ref[base + k * LANES : base + (k + 1) * LANES, :] for k in range(3)], axis=1
    )
    base = 11 * LANES
    widen = table_ref[base : base + 3 * tall, :]
    base = base + 3 * tall
    for e in range(cap_x):
        keep = inside & (e < wx)
        squares[8 * e : 8 * e + cap_y, 0:layers] = jnp.where(keep, diff_ref[e], 0.0)
        sq_kappa[8 * e : 8 * e + cap_y, 0:layers] = jnp.where(keep, kappa_ref[e], 0.0)
    deep = jnp.dot(squares[...], depth_table, precision=HIGHEST, preferred_element_type=jnp.float32)
    deep_kappa = jnp.dot(
        sq_kappa[...], depth_table[:, 0:LANES], precision=HIGHEST, preferred_element_type=jnp.float32
    )
    big = jnp.dot(
        widen[0:tall, :],
        jnp.concatenate([deep, deep_kappa], axis=1),
        precision=HIGHEST,
        preferred_element_type=jnp.float32,
    )
    both = jnp.dot(
        widen[tall : 3 * tall, :],
        deep[:, 0:LANES],
        precision=HIGHEST,
        preferred_element_type=jnp.float32,
    )
    for ref in (e_px, e_ya, e_yb):
        ref[0:ROWS, :] = zero_plane
        ref[tall + ROWS : tall + 2 * ROWS, :] = zero_plane
    for edge in (0, tall + ROWS):
        e_big[edge : edge + ROWS, :] = jnp.zeros((ROWS, 3 * LANES), jnp.float32)
    e_px[ROWS : ROWS + tall, :] = big[:, 0:LANES]
    e_big[ROWS : ROWS + tall, :] = big[:, LANES : 4 * LANES]
    e_ya[ROWS : ROWS + tall, :] = both[0:tall]
    e_yb[ROWS : ROWS + tall, :] = both[tall : 2 * tall]

    fields = (f_z, f_im, f_inv, f_mass, f_ya, f_yb, f_za, f_zb)
    for ref in fields:
        for x in range(7 * cap_x, PLANES):
            ref[x * ROWS : (x + 1) * ROWS, :] = zero_plane

    sources = (
        (f_za, e_big, 0), (f_zb, e_big, 1), (f_mass, e_big, 2), (f_ya, e_ya, 0), (f_yb, e_yb, 0),
    )
    row_factor = table_ref[base : base + ROWS, :]
    depth_factor = table_ref[base + ROWS : base + ROWS + 1, :]
    corner = float(STIFF[7, 7])

    def fill_plane(x, e, b):
        values = []
        for target, source, lane in sources:
            lanes = slice(lane * LANES, (lane + 1) * LANES)
            value = float(WEIGHTS[b]) * source[plane(e + 1), lanes]
            if b == 0:
                value = value + float(WEIGHTS[7]) * source[plane(e), lanes]
            target[plane(x), :] = value
            values.append(value)
        za, zb, mass, ya, yb = values
        diagonal = mass + ya * row_factor + yb * corner + za * depth_factor + zb * corner
        diagonal = diagonal + float(STIFF[b, b]) * e_px[plane(e + 1), :]
        if b == 0:
            diagonal = diagonal + float(STIFF[7, 7]) * e_px[plane(e), :]
        f_inv[plane(x), :] = diagonal

    def fill(e, _):
        for b in range(7):
            fill_plane(7 * e + b, e, b)
        return 0

    lax.fori_loop(0, cap_x, fill, 0)
    fill_plane(7 * cap_x, cap_x, 0)

    deep_node, deep_lane = iota((LANES, LANES), 0), iota((LANES, LANES), 1)
    for dy in (-1, 0, 1):
        part = slice((dy + 1) * LANES, (dy + 2) * LANES)
        start = (bj + 1 + dy) * 16
        gather_map[part, :] = flag(deep_lane == start + deep_node // 8).astype(jnp.bfloat16)
        spread_map[:, part] = flag(deep_node == start + deep_lane // 8).astype(jnp.bfloat16)
    grid_row = iota((8, LANES), 0)
    row32 = iota((ROWS, LANES), 0)
    chunk = 4 * ROWS
    chunks = (7 * cap_x + 4) // 4

    def coarse_sums(ref, assembled):
        def add(i, value):
            return value + jnp.sum(
                ref[pl.ds(pl.multiple_of(i * chunk, chunk), chunk), :].reshape(4, ROWS, LANES), axis=0
            )

        middle = lax.fori_loop(0, chunks, add, zero_plane, unroll=True)
        low, high = 0.5 * has_left * ref[0:ROWS, :], 0.5 * has_right * high_plane(ref)
        sums = [jnp.zeros((8, LANES), jnp.float32)] * 3
        middle = middle - low - high
        for dx, value in ((0, middle),) if assembled else ((-1, low), (0, middle), (1, high)):
            below = 0.5 * has_below * value[0:1, :]
            above = 0.5 * has_above * high_row(value)
            centre = jnp.sum(value, axis=0, keepdims=True) - below - above
            for k, profile in ((1, centre),) if assembled else enumerate((below, centre, above)):
                sums[k] = sums[k] + jnp.where(grid_row == bi + 1 + dx, profile, 0.0)
        return exact_dot(jnp.concatenate(sums, axis=1), gather_map[...])

    def wait_in(buffer, count, send, recv):
        part = buffer.at[pl.ds(0, count)]
        remote(part, part, send, recv, beside(1, 0)).wait_recv()

    def wait_out(buffer, count, send, recv):
        part = buffer.at[pl.ds(0, count)]
        remote(part, part, send, recv, beside(1, 0)).wait_send()

    def exchange_start(source, target, count, me, device, send, recv):
        def go(o, _):
            remote(source, target.at[me], send, recv, device(lax.rem(me + o, count))).start()
            return 0

        lax.fori_loop(1, count, go, 0, unroll=True)
        target[me] = source[...]

    def reduce_start(a, ref, assembled=False):
        grid_s[a] = coarse_sums(ref, assembled)
        exchange_start(
            grid_s.at[a], grid_r.at[a], near, mine, in_block, r_send.at[a, 0], r_recv.at[a, 0]
        )

    lane = iota((1, LANES), 1)

    def scalar_row(values):
        result = jnp.zeros((1, LANES), jnp.float32)
        for i, value in enumerate(values):
            result = jnp.where(lane == i, value, result)
        return result

    def pick(values, i):
        return total(jnp.where(lane == i, values, 0.0))

    grid_rows, grid_lanes = bx + 2, (by + 2) * 16

    def reduce_middle(a, scalars, inner=False):
        wait_in(grid_r.at[a], near - 1, r_send.at[a, 0], r_recv.at[a, 0])
        turned = jnp.sum(grid_r[a], axis=0).T
        value = jnp.zeros((8, width), jnp.float32)
        rim = 1 if inner else 0
        part = slice(16 * rim, grid_lanes - 16 * rim)
        for i in range(rim, grid_rows - rim):
            product = rows_x[i, part, :] * turned[part, i : i + 1]
            value = value + jnp.sum(product.reshape(-1, 8, width), axis=0)
        value = jnp.sum(value, axis=0, keepdims=True)
        for g in range(groups):
            chunk_s[a, g : g + 1, :] = value[:, g * LANES : (g + 1) * LANES]
        chunk_s[a, groups : groups + 1, :] = scalar_row(scalars)
        exchange_start(
            chunk_s.at[a], chunk_r.at[a], far, block_id, across, r_send.at[a, 1], r_recv.at[a, 1]
        )

    def reduce_finish(a, extra):
        wait_in(chunk_r.at[a], far - 1, r_send.at[a, 1], r_recv.at[a, 1])
        sums = jnp.sum(chunk_r[a], axis=0)
        through = sums[0:groups, :]
        turned = jnp.zeros((grid_lanes, LANES), jnp.float32)
        wide_lane = iota((grid_lanes, LANES), 1)
        for i in range(grid_rows):
            product = rows_x[i, :, 0:LANES] * through[0:1, :]
            for g in range(1, groups):
                product = product + rows_x[i, :, g * LANES : (g + 1) * LANES] * through[g : g + 1, :]
            turned = jnp.where(wide_lane == i, jnp.sum(product, axis=1, keepdims=True), turned)
        turned = jnp.concatenate(
            [turned, jnp.zeros((LANES - grid_lanes, LANES), jnp.float32)], axis=0
        )
        scalars = sums[groups : groups + 1, :]
        if extra is not None:
            scalars = jnp.where(lane == 8, extra, scalars)
        back_s[a] = jnp.where(grid_row == 7, scalars, turned.T[0:8, :])
        exchange_start(
            back_s.at[a], back_r.at[a], near, mine, in_block, r_send.at[a, 2], r_recv.at[a, 2]
        )
        wait_in(back_r.at[a], near - 1, r_send.at[a, 2], r_recv.at[a, 2])
        grid = jnp.sum(back_r[a], axis=0)
        wait_out(grid_r.at[a], near - 1, r_send.at[a, 0], r_recv.at[a, 0])
        wait_out(chunk_r.at[a], far - 1, r_send.at[a, 1], r_recv.at[a, 1])
        wait_out(back_r.at[a], near - 1, r_send.at[a, 2], r_recv.at[a, 2])
        return grid, grid[7:8, :], through

    def coarse_planes(grid):
        deep_values = exact_dot(grid, spread_map[...])

        def spread(dx):
            line = jnp.sum(jnp.where(iota((8, 3 * LANES), 0) == bi + 1 + dx, deep_values, 0.0), axis=0, keepdims=True)
            below, centre, above = (line[:, k * LANES : (k + 1) * LANES] for k in range(3))
            value = jnp.where(row32 == 0, centre + 0.5 * has_below * (below - centre), centre)
            return jnp.where(row32 == end_y, value + 0.5 * has_above * (above - centre), value)

        middle = spread(0)
        first = middle + 0.5 * has_left * (spread(-1) - middle)
        second = middle + 0.5 * has_right * (spread(1) - middle)
        return first, middle, second

    def coarse_at(x, planes):
        first, middle, second = planes
        return jnp.where(x == 0, first, jnp.where(x == end_x, second, middle))

    def apply_operator():
        def along_x(e, carried):
            values = [f_z[plane(7 * e + c), :] for c in range(8)]
            sums = [values[c] + values[7 - c] for c in range(4)]
            gaps = [values[c] - values[7 - c] for c in range(4)]
            scale = e_px[plane(e + 1), :]
            results = [None] * 8
            for b in range(4):
                even = sum(float(0.5 * (STIFF[b, c] + STIFF[b, 7 - c])) * sums[c] for c in range(4))
                odd = sum(float(0.5 * (STIFF[b, c] - STIFF[b, 7 - c])) * gaps[c] for c in range(4))
                results[b] = scale * (even + odd)
                results[7 - b] = scale * (even - odd)
            f_im[plane(7 * e), :] = carried + results[0]
            for b in range(1, 7):
                f_im[plane(7 * e + b), :] = results[b]
            return results[7]

        carried = lax.fori_loop(0, cap_x, along_x, zero_plane, unroll=True)
        f_im[plane(7 * cap_x), :] = carried

        def along_rest(i, product):
            rows = pl.ds(pl.multiple_of(i * chunk, chunk), chunk)
            value = f_z[rows, :]
            high = value.astype(jnp.bfloat16)
            low = (value - high.astype(jnp.float32)).astype(jnp.bfloat16)
            deep = jnp.dot(
                jnp.concatenate([high, low, high], axis=1),
                vertical_ref[...],
                preferred_element_type=jnp.float32,
            )
            wide = jnp.dot(
                across_ref[...],
                jnp.concatenate([high, low, high], axis=0),
                preferred_element_type=jnp.float32,
            )
            image = f_im[rows, :] + f_mass[rows, :] * value
            image = image + f_ya[rows, :] * wide[0:chunk] + f_yb[rows, :] * wide[chunk:]
            image = image + f_za[rows, :] * deep[:, 0:LANES] + f_zb[rows, :] * deep[:, LANES:]
            f_im[rows, :] = image
            return product + jnp.sum((value * image).reshape(chunk // 8, 8, LANES), axis=0)

        product = lax.fori_loop(0, chunks, along_rest, jnp.zeros((8, LANES), jnp.float32), unroll=True)
        return total(product)

    diagonal_copies = halo_start(1, f_inv)
    halo_finish(0, f_r, load_copies)
    reduce_start(0, f_r, True)

    own_rows.wait()

    def scatter_wait(o, _):
        scatter_copy(o).wait()
        return 0

    lax.fori_loop(1, near, scatter_wait, 0)
    spans = {1: (slice(bx, bx + 1), slice(0, 1)), -1: (slice(1, 2), slice(bx + 1, bx + 2))}
    spans[0] = (slice(1, bx + 1), slice(1, bx + 1))
    across_spans = {1: (by, 0, 1), -1: (1, by + 1, 1), 0: (1, 1, by)}
    ring = []
    for k, (dx, dy) in enumerate(DIRECTIONS):
        (source_x, target_x), (source_y, target_y, count) = spans[dx], across_spans[dy]
        copy = remote(
            rows_x.at[source_x, pl.ds(source_y * 16, count * 16), :],
            rows_x.at[target_x, pl.ds(target_y * 16, count * 16), :],
            ring_send.at[k],
            ring_recv.at[k],
            beside(dx * bx, dy * by),
        )
        ring.append(copy)

    halo_finish(1, f_inv, diagonal_copies)
    share_low = jnp.where(row32 == 0, 1.0 - 0.5 * has_below, 1.0)
    share_row = jnp.where(row32 == end_y, 1.0 - 0.5 * has_above, share_low)

    def share_x(x):
        low = jnp.where(x == 0, 1.0 - 0.5 * has_left, 1.0)
        return jnp.where(x == end_x, 1.0 - 0.5 * has_right, low)

    def invert(x, value):
        diagonal = f_inv[plane(x), :]
        inverse = jnp.where(diagonal > 0.0, 1.0 / jnp.where(diagonal > 0.0, diagonal, 1.0), 0.0)
        f_inv[plane(x), :] = inverse
        share = jnp.where(diagonal > 0.0, share_row * share_x(x), 0.0)
        f_share[plane(x), :] = share
        resid = f_r[plane(x), :]
        f_sol[plane(x), :] = zero_plane
        f_w[plane(x), :] = zero_plane
        f_d[plane(x), :] = zero_plane
        return value + share * inverse * resid * resid

    planes = 7 * cap_x + 1
    jacobi = total(lax.fori_loop(0, planes, invert, zero_plane))
    for copy in ring[2:4]:
        copy.start()
    reduce_middle(0, [], True)
    for copy in ring[0:2] + ring[4:]:
        copy.start()
    for copy in ring:
        copy.wait()
    grid, _, through = reduce_finish(0, None)
    coarse = coarse_planes(grid)

    def begin(x, _):
        inverse = f_inv[plane(x), :]
        value = jnp.where(inverse > 0.0, coarse_at(x, coarse), 0.0)
        f_z[plane(x), :] = inverse * f_r[plane(x), :] + value
        return 0

    lax.fori_loop(0, planes, begin, 0)

    cross = jnp.zeros((1, 1), jnp.float32)
    beta, rho, curvature = cross, None, cross
    through_w, grid_w = jnp.zeros_like(through), jnp.zeros_like(grid)

    def scalars_of(values, squared):
        rho_now = pick(values, 2) + squared
        beta_now = jnp.zeros((1, 1), jnp.float32) if rho is None else rho_now / rho
        bent = pick(values, 0) + 2.0 * beta_now * pick(values, 1) + beta_now * beta_now * curvature
        return rho_now, beta_now, bent

    for i in range(ITERS):
        own = apply_operator()
        squared = total(through * through)
        if i + 1 < ITERS:
            reduce_start(i + 1, f_im)
            image_copies = halo_start(2 + i, f_im)
            reduce_middle(i + 1, [own, cross, jacobi])
            halo_finish(2 + i, f_im, image_copies)
            grid_q, values, through_q = reduce_finish(i + 1, squared)
            rho, beta, curvature = scalars_of(values, pick(values, 8))
            step = rho / curvature
            grid_w = grid_q + beta * grid_w
            through_w = through_q + beta * through_w
            grid = grid - step * grid_w
            through = through - step * through_w
            coarse = coarse_planes(grid)

            def advance(x, sums):
                here = plane(x)
                old = f_z[here, :]
                direction = old + beta * f_d[here, :]
                image = f_im[here, :] + beta * f_w[here, :]
                f_d[here, :] = direction
                f_w[here, :] = image
                f_sol[here, :] = f_sol[here, :] + step * direction
                resid = f_r[here, :] - step * image
                f_r[here, :] = resid
                scaled = f_inv[here, :] * resid
                share = f_share[here, :]
                value = scaled + jnp.where(share > 0.0, coarse_at(x, coarse), 0.0)
                f_z[here, :] = value
                return sums[0] + share * scaled * resid, sums[1] + share * value * image

            jacobi, cross = lax.fori_loop(
                0, planes, advance, (zero_plane, zero_plane), unroll=True
            )
            jacobi, cross = total(jacobi), total(cross)
        else:
            last_s[...] = scalar_row([own, cross, jacobi])
            exchange_start(last_s, last_r, far, block_id, across, l_send.at[0], l_recv.at[0])
            image_copies = halo_start(2 + i, f_im)
            halo_finish(2 + i, f_im, image_copies)
            wait_in(last_r, far - 1, l_send.at[0], l_recv.at[0])
            end_s[...] = jnp.where(lane == 8, squared, jnp.sum(last_r[...], axis=0))
            exchange_start(end_s, end_r, near, mine, in_block, l_send.at[1], l_recv.at[1])
            wait_in(end_r, near - 1, l_send.at[1], l_recv.at[1])
            values = jnp.sum(end_r[...], axis=0)
            rho, beta, curvature = scalars_of(values, pick(values, 8))
            step = rho / curvature
            wait_out(last_r, far - 1, l_send.at[0], l_recv.at[0])
            wait_out(end_r, near - 1, l_send.at[1], l_recv.at[1])

    def put(target, x, value):
        last = high_row(value)
        rows = value[0:slots_y, :]
        rows = jnp.where(row < end_y, rows, jnp.where(row == slots_y - 1, last, 0.0))
        target[x] = rows

    def finish(x, _):
        here = plane(x)
        found = f_sol[here, :] + step * (f_z[here, :] + beta * f_d[here, :])
        resid = f_r[here, :] - step * (f_im[here, :] + beta * f_w[here, :])
        f_sol[here, :] = found
        f_r[here, :] = resid
        put(solution_ref, x, jnp.where(x < end_x, found, 0.0))
        put(residual_ref, x, jnp.where(x < end_x, resid, 0.0))
        return 0

    lax.fori_loop(0, planes, finish, 0)
    put(solution_ref, slots_x - 1, high_plane(f_sol))
    put(residual_ref, slots_x - 1, high_plane(f_r))


def body(nx, ny, right_side, diffusion, kappa, widths_x, widths_y, factor):
    cap_x, cap_y, layers = diffusion.shape
    bx, by = BLOCK, BLOCK
    near, far = bx * by, (nx // bx) * (ny // by)
    groups = factor.shape[1] // (near * LANES)
    f32, bf16 = jnp.float32, jnp.bfloat16
    smem = pl.BlockSpec(memory_space=pltpu.SMEM)
    vmem = pl.BlockSpec(memory_space=pltpu.VMEM)
    hbm = pl.BlockSpec(memory_space=pltpu.HBM)
    tall = cap_x * ROWS
    dma = pltpu.SemaphoreType.DMA
    table = jnp.asarray(tables(cap_x, cap_y, layers))

    def room(*shape, dtype=f32):
        return pltpu.VMEM(shape, dtype)

    scratch = [room(*array.shape) for array in (right_side, diffusion, kappa, table)]
    scratch += [room(3 * LANES, 2 * LANES, dtype=bf16), room(2 * LANES, 3 * LANES, dtype=bf16)]
    scratch += [room(PLANES * ROWS, LANES)] * 13
    scratch += [
        room(tall + 2 * ROWS, LANES),
        room(tall + 2 * ROWS, 3 * LANES),
        room(tall + 2 * ROWS, LANES),
        room(tall + 2 * ROWS, LANES),
        room(LANES, LANES),
        room(LANES, LANES),
        room(bx + 2, (by + 2) * 16, groups * LANES),
        room(3 * LANES, LANES, dtype=bf16),
        room(LANES, 3 * LANES, dtype=bf16),
    ]
    halos = 2 + ITERS
    for _ in range(2):
        scratch += [
            room(halos, 2, ROWS, LANES),
            room(halos, 2, PLANES, LANES),
            room(halos, 4, 8, LANES),
        ]
    scratch += [
        room(ITERS, 8, LANES),
        room(ITERS, near, 8, LANES),
        room(ITERS, groups + 1, LANES),
        room(ITERS, far, groups + 1, LANES),
        room(ITERS, 8, LANES),
        room(ITERS, near, 8, LANES),
        room(1, LANES),
        room(far, 1, LANES),
        room(1, LANES),
        room(near, 1, LANES),
        dma((4,)), dma((1,)), dma((near,)), dma((near,)), dma((8,)), dma((8,)),
        dma((halos, 8)), dma((halos, 8)), dma((ITERS, 3)), dma((ITERS, 3)), dma((2,)), dma((2,)),
    ]
    shape = pltpu.VMEM(right_side.shape, f32)
    return pl.pallas_call(
        functools.partial(kernel, nx, ny, cap_x, cap_y, layers, bx, by),
        out_shape=(shape, shape),
        in_specs=[smem, smem] + [hbm] * 5,
        out_specs=(vmem, vmem),
        scratch_shapes=scratch,
        compiler_params=pltpu.CompilerParams(
            collective_id=0, has_side_effects=True, vmem_limit_bytes=56 * 1024 * 1024
        ),
    )(widths_x, widths_y, right_side, diffusion, kappa, factor, table)


def solution(mesh):
    nx, ny = mesh.shape["gx"], mesh.shape["gy"]
    in_specs = (
        P("gx", "gy", None),
        P("gx", "gy", None),
        P("gx", "gy", None),
        P("gx"),
        P("gy"),
        P(("gx", "gy"), None),
    )
    out_specs = (P("gx", "gy", None), P("gx", "gy", None))
    return jax.shard_map(
        functools.partial(body, nx, ny),
        mesh=mesh,
        in_specs=in_specs,
        out_specs=out_specs,
        check_vma=False,
    )
```

```python
import functools

import jax
import jax.numpy as jnp
import ml_dtypes
import numpy as np
from jax import lax
from jax.experimental import pallas as pl
from jax.experimental.pallas import tpu as pltpu
from jax.sharding import PartitionSpec as P

ITERS = 3
HIGHEST = lax.Precision.HIGHEST
MESH = pl.DeviceIdType.MESH
LANES = 128
ROWS = 32
PLANES = 48
BLOCK = 4
DIRECTIONS = [(1, 0), (-1, 0), (0, 1), (0, -1), (1, 1), (1, -1), (-1, 1), (-1, -1)]


def gll_weights():
    return np.array(
        [
            1.0 / 28.0,
            0.2107042271435061,
            0.3411226924835044,
            0.4124587946587038,
            0.4124587946587038,
            0.3411226924835044,
            0.2107042271435061,
            1.0 / 28.0,
        ]
    )


def gll_derivative():
    points = np.array(
        [
            -1.0,
            -0.8717401485096066,
            -0.5917001814331423,
            -0.2092992179024789,
            0.2092992179024789,
            0.5917001814331423,
            0.8717401485096066,
            1.0,
        ]
    )
    identity = np.eye(8) > 0
    spacing = np.where(identity, 1.0, points[:, None] - points[None, :])
    barycentric = 1.0 / np.prod(spacing, axis=1)
    matrix = np.where(identity, 0.0, barycentric[None, :] / barycentric[:, None] / spacing)
    return np.where(identity, -np.sum(matrix, axis=1)[:, None], matrix)


WEIGHTS = gll_weights()
STIFF = gll_derivative().T @ np.diag(WEIGHTS) @ gll_derivative()


def split(matrix):
    high = matrix.astype(ml_dtypes.bfloat16)
    low = (matrix - high.astype(np.float64)).astype(ml_dtypes.bfloat16)
    return high, low


def band(cells, size):
    first, second = np.zeros((size, size)), np.zeros((size, size))
    for e in range(cells):
        for b in range(7):
            first[7 * e + b, 7 * e : 7 * e + 8] = STIFF[b]
        second[7 * e + 7, 7 * e : 7 * e + 8] = STIFF[7]
    return first, second


def tables(cap_x, cap_y, layers):
    first, second = band(layers, LANES)
    vertical = split(np.concatenate([first, second], axis=0).T)
    first, second = band(cap_y, ROWS)
    stacked = np.concatenate([np.kron(np.eye(4), first), np.kron(np.eye(4), second)], axis=0)
    across = split(stacked)
    depth = np.zeros((LANES, 3 * LANES))
    for h in range(layers):
        depth[h, 7 * h : 7 * h + 8] = WEIGHTS
        depth[h, LANES + 7 * h : LANES + 7 * h + 7] = 1.0
        depth[h, 2 * LANES + 7 * h + 7] = 1.0
    weigh, pick, ends = np.zeros((ROWS, 8)), np.zeros((ROWS, 8)), np.zeros((ROWS, 8))
    for f in range(cap_y):
        weigh[7 * f : 7 * f + 8, f] = WEIGHTS
        pick[7 * f : 7 * f + 7, f] = 1.0
        ends[7 * f + 7, f] = 1.0
    unit = np.eye(cap_x)
    widen = np.concatenate([np.kron(unit, weigh), np.kron(unit, pick), np.kron(unit, ends)], axis=0)
    widen = np.pad(widen, ((0, 0), (0, LANES - widen.shape[1])))
    factor = np.zeros((ROWS + 8, LANES))
    factor[: 7 * cap_y] = STIFF[np.arange(7 * cap_y) % 7, np.arange(7 * cap_y) % 7][:, None]
    factor[ROWS:, : 7 * layers] = STIFF[np.arange(7 * layers) % 7, np.arange(7 * layers) % 7][None, :]
    parts = [half for part in vertical for half in (part[:, :LANES], part[:, LANES:])]
    parts += [*across]
    parts += [depth[:, k * LANES : (k + 1) * LANES] for k in range(3)] + [widen, factor]
    return np.concatenate([part.astype(np.float32) for part in parts], axis=0)


def plane(x):
    return pl.ds(pl.multiple_of(x * ROWS, ROWS), ROWS)


def total(values):
    return jnp.sum(values, axis=(0, 1), keepdims=True)


def iota(shape, dim):
    return lax.broadcasted_iota(jnp.int32, shape, dim)


def pieces(values):
    first = values.astype(jnp.bfloat16)
    rest = values - first.astype(jnp.float32)
    second = rest.astype(jnp.bfloat16)
    third = (rest - second.astype(jnp.float32)).astype(jnp.bfloat16)
    return [first, second, third]


def exact_dot(values, chosen):
    rows = values.shape[0]
    result = jnp.dot(
        jnp.concatenate(pieces(values), axis=0), chosen, preferred_element_type=jnp.float32
    )
    return result[0:rows] + result[rows : 2 * rows] + result[2 * rows : 3 * rows]


def kernel(
    nx, ny, cap_x, cap_y, layers, bx, by,
    wx_ref, wy_ref, load_any, diff_any, kappa_any, factor_any,
    table_any,
    solution_ref, residual_ref,
    load_ref, diff_ref, kappa_ref, table_ref, vertical_ref, across_ref,
    f_z, f_im, f_w, f_d, f_r, f_sol, f_inv, f_share, f_mass, f_ya, f_yb, f_za, f_zb,
    e_px, e_big, e_ya, e_yb, squares, sq_kappa,
    rows_x, gather_map, spread_map,
    halo_sx, halo_sy, halo_sc, halo_rx, halo_ry, halo_rc,
    grid_s, grid_r, chunk_s, chunk_r, back_s, back_r, last_s, last_r, end_s, end_r, line_s, line_r,
    in_sem, own_sem, x_send, x_recv, ring_send, ring_recv,
    h_send, h_recv, r_send, r_recv, l_send, l_recv, line_send, line_recv,
):
    p, q = lax.axis_index("gx"), lax.axis_index("gy")
    wx, wy = wx_ref[0], wy_ref[0]
    groups = chunk_s.shape[1] - 1
    width = groups * LANES
    end_x, end_y = 7 * wx, 7 * wy
    near, far = bx * by, (nx // bx) * (ny // by)
    ax, ay = nx // bx, ny // by
    bi, bj, ai, aj = lax.rem(p, bx), lax.rem(q, by), p // bx, q // by
    mine, block_id = bi * by + bj, ai * ay + aj

    def beside(dx, dy):
        return (lax.rem(p + dx + nx, nx), lax.rem(q + dy + ny, ny))

    def in_block(index):
        return (ai * bx + index // by, aj * by + lax.rem(index, by))

    def across(index):
        return (index // ay * bx + bi, lax.rem(index, ay) * by + bj)

    barrier = pltpu.get_barrier_semaphore()

    def greet(device):
        pl.semaphore_signal(barrier, inc=1, device_id=device, device_id_type=MESH)

    def greet_near(o, _):
        greet(in_block(lax.rem(mine + o, near)))
        return 0

    def greet_far(o, _):
        greet(across(lax.rem(block_id + o, far)))
        return 0

    lax.fori_loop(1, near, greet_near, 0, unroll=True)
    lax.fori_loop(1, far, greet_far, 0, unroll=True)
    for dx, dy in DIRECTIONS:
        greet(beside(dx, dy))

    arrivals = []
    for i, (source, target) in enumerate((
        (diff_any, diff_ref), (kappa_any, kappa_ref), (table_any, table_ref), (load_any, load_ref),
    )):
        copy = pltpu.make_async_copy(source, target, in_sem.at[i])
        copy.start()
        arrivals.append(copy)

    def remote(source, target, send, recv, device):
        return pltpu.make_async_remote_copy(
            src_ref=source,
            dst_ref=target,
            send_sem=send,
            recv_sem=recv,
            device_id=device,
            device_id_type=MESH,
        )

    def columns(index):
        return pl.ds(pl.multiple_of(index * width, LANES), width)

    def rows_of(j):
        return pl.ds(pl.multiple_of((j + 1) * 16, 16), 16)

    own_rows = pltpu.make_async_copy(
        factor_any.at[:, columns(mine)], rows_x.at[bi + 1, rows_of(bj), :], own_sem.at[0]
    )
    own_rows.start()

    def flag(condition):
        return jnp.where(condition, 1.0, 0.0).astype(jnp.float32)

    has_left, has_right = flag(p > 0), flag(p < nx - 1)
    has_below, has_above = flag(q > 0), flag(q < ny - 1)

    def scatter_copy(o):
        peer = lax.rem(mine + o, near)
        return remote(
            factor_any.at[:, columns(peer)],
            rows_x.at[bi + 1, rows_of(bj), :],
            x_send.at[o],
            x_recv.at[o],
            in_block(peer),
        )

    def scatter(o, _):
        scatter_copy(o).start()
        return 0

    zero_plane = jnp.zeros((ROWS, LANES), jnp.float32)
    slots_x, slots_y = load_ref.shape[0], load_ref.shape[1]
    row = iota((slots_y, LANES), 0)
    real = iota((slots_y, LANES), 1) <= 7 * layers
    f_r[...] = jnp.zeros_like(f_r)
    arrivals[3].wait()

    def take(x, _):
        value = jnp.where(x < end_x, load_ref[x], jnp.where(x == end_x, load_ref[slots_x - 1], 0.0))
        last = value[slots_y - 1 : slots_y, :]
        value = jnp.where(row < end_y, value, jnp.where(row == end_y, last, 0.0))
        f_r[pl.ds(pl.multiple_of(x * ROWS, ROWS), slots_y), :] = jnp.where(real, value, 0.0)
        return 0

    lax.fori_loop(0, slots_x, take, 0)

    def high_plane(ref):
        value = jnp.zeros((ROWS, LANES), jnp.float32)
        for j in range(1, cap_x + 1):
            value = value + jnp.where(wx == j, ref[7 * j * ROWS : (7 * j + 1) * ROWS, :], 0.0)
        return value

    def side(j):
        return pl.ds(7 * j, PLANES, stride=ROWS)

    def high_row(plane_value):
        value = jnp.zeros((1, LANES), jnp.float32)
        for j in range(1, cap_y + 1):
            value = value + jnp.where(wy == j, plane_value[7 * j : 7 * j + 1, :], 0.0)
        return value

    def halo_copies(h):
        copies = []
        for k, (dx, dy) in enumerate(DIRECTIONS):
            if dy == 0:
                slot = (h, 0 if dx > 0 else 1)
                source, target = halo_sx.at[slot], halo_rx.at[slot]
            elif dx == 0:
                slot = (h, 0 if dy > 0 else 1)
                source, target = halo_sy.at[slot], halo_ry.at[slot]
            else:
                source, target = halo_sc.at[h, k - 4], halo_rc.at[h, k - 4]
            copies.append(remote(source, target, h_send.at[h, k], h_recv.at[h, k], beside(dx, dy)))
        return copies

    def halo_pack(h, ref):
        low, high = ref[0:ROWS, :], high_plane(ref)
        halo_sx[h, 0] = high
        halo_sx[h, 1] = low
        above = jnp.zeros((PLANES, LANES), jnp.float32)
        for j in range(1, cap_y + 1):
            above = above + jnp.where(wy == j, ref[side(j), :], 0.0)
        halo_sy[h, 0] = above
        halo_sy[h, 1] = ref[side(0), :]
        rows = (high_row(high), high[0:1, :], high_row(low), low[0:1, :])
        for k, value in enumerate(rows):
            halo_sc[h, k] = jnp.broadcast_to(value, (8, LANES))

    def halo_send(h):
        copies = halo_copies(h)
        for copy in copies:
            copy.start()
        return copies

    def halo_start(h, ref):
        halo_pack(h, ref)
        return halo_send(h)

    place = iota((PLANES, LANES), 0)

    def halo_finish(h, ref, copies):
        for copy in copies:
            copy.wait()
        ref[0:ROWS, :] = ref[0:ROWS, :] + has_left * halo_rx[h, 0]
        from_right = has_right * halo_rx[h, 1]
        for j in range(1, cap_x + 1):
            rows = slice(7 * j * ROWS, (7 * j + 1) * ROWS)
            ref[rows, :] = ref[rows, :] + jnp.where(wx == j, from_right, 0.0)

        def line(side_value, first, second):
            side_value = side_value + jnp.where(place == 0, has_left * first[0:1, :], 0.0)
            return side_value + jnp.where(place == end_x, has_right * second[0:1, :], 0.0)

        below = has_below * line(halo_ry[h, 0], halo_rc[h, 0], halo_rc[h, 2])
        above = has_above * line(halo_ry[h, 1], halo_rc[h, 1], halo_rc[h, 3])
        ref[side(0), :] = ref[side(0), :] + below
        for j in range(1, cap_y + 1):
            ref[side(j), :] = ref[side(j), :] + jnp.where(wy == j, above, 0.0)

    halo_pack(0, f_r)
    pl.semaphore_wait(barrier, near + far - 2 + len(DIRECTIONS))

    load_copies = halo_send(0)
    lax.fori_loop(1, near, scatter, 0, unroll=True)

    squares[...] = jnp.zeros_like(squares)
    sq_kappa[...] = jnp.zeros_like(sq_kappa)
    for copy in arrivals[0:3]:
        copy.wait()
    inside = iota((cap_y, layers), 0) < wy
    tall = cap_x * ROWS
    base = 4 * LANES
    for g in range(2):
        lanes = slice(g * LANES, (g + 1) * LANES)
        high = table_ref[g * LANES : (g + 1) * LANES, :].astype(jnp.bfloat16)
        low = table_ref[(g + 2) * LANES : (g + 3) * LANES, :].astype(jnp.bfloat16)
        for k, part in enumerate((high, high, low)):
            vertical_ref[k * LANES : (k + 1) * LANES, lanes] = part
    high = table_ref[base : base + 2 * LANES, :].astype(jnp.bfloat16)
    low = table_ref[base + 2 * LANES : base + 4 * LANES, :].astype(jnp.bfloat16)
    for k, part in enumerate((high, high, low)):
        across_ref[:, k * LANES : (k + 1) * LANES] = part
    base = 8 * LANES
    depth_table = jnp.concatenate(
        [table_ref[base + k * LANES : base + (k + 1) * LANES, :] for k in range(3)], axis=1
    )
    base = 11 * LANES
    widen = table_ref[base : base + 3 * tall, :]
    base = base + 3 * tall
    for e in range(cap_x):
        keep = inside & (e < wx)
        squares[8 * e : 8 * e + cap_y, 0:layers] = jnp.where(keep, diff_ref[e], 0.0)
        sq_kappa[8 * e : 8 * e + cap_y, 0:layers] = jnp.where(keep, kappa_ref[e], 0.0)
    deep = jnp.dot(squares[...], depth_table, precision=HIGHEST, preferred_element_type=jnp.float32)
    deep_kappa = jnp.dot(
        sq_kappa[...], depth_table[:, 0:LANES], precision=HIGHEST, preferred_element_type=jnp.float32
    )
    big = jnp.dot(
        widen[0:tall, :],
        jnp.concatenate([deep, deep_kappa], axis=1),
        precision=HIGHEST,
        preferred_element_type=jnp.float32,
    )
    both = jnp.dot(
        widen[tall : 3 * tall, :],
        deep[:, 0:LANES],
        precision=HIGHEST,
        preferred_element_type=jnp.float32,
    )
    for ref in (e_px, e_ya, e_yb):
        ref[0:ROWS, :] = zero_plane
        ref[tall + ROWS : tall + 2 * ROWS, :] = zero_plane
    for edge in (0, tall + ROWS):
        e_big[edge : edge + ROWS, :] = jnp.zeros((ROWS, 3 * LANES), jnp.float32)
    e_px[ROWS : ROWS + tall, :] = big[:, 0:LANES]
    e_big[ROWS : ROWS + tall, :] = big[:, LANES : 4 * LANES]
    e_ya[ROWS : ROWS + tall, :] = both[0:tall]
    e_yb[ROWS : ROWS + tall, :] = both[tall : 2 * tall]

    fields = (f_z, f_im, f_inv, f_mass, f_ya, f_yb, f_za, f_zb)
    for ref in fields:
        for x in range(7 * cap_x, PLANES):
            ref[x * ROWS : (x + 1) * ROWS, :] = zero_plane

    sources = (
        (f_za, e_big, 0), (f_zb, e_big, 1), (f_mass, e_big, 2), (f_ya, e_ya, 0), (f_yb, e_yb, 0),
    )
    row_factor = table_ref[base : base + ROWS, :]
    depth_factor = table_ref[base + ROWS : base + ROWS + 1, :]
    corner = float(STIFF[7, 7])

    def fill_plane(x, e, b):
        values = []
        for target, source, lane in sources:
            lanes = slice(lane * LANES, (lane + 1) * LANES)
            value = float(WEIGHTS[b]) * source[plane(e + 1), lanes]
            if b == 0:
                value = value + float(WEIGHTS[7]) * source[plane(e), lanes]
            target[plane(x), :] = value
            values.append(value)
        za, zb, mass, ya, yb = values
        diagonal = mass + ya * row_factor + yb * corner + za * depth_factor + zb * corner
        diagonal = diagonal + float(STIFF[b, b]) * e_px[plane(e + 1), :]
        if b == 0:
            diagonal = diagonal + float(STIFF[7, 7]) * e_px[plane(e), :]
        f_inv[plane(x), :] = diagonal

    def fill(e, _):
        for b in range(7):
            fill_plane(7 * e + b, e, b)
        return 0

    lax.fori_loop(0, cap_x, fill, 0)
    fill_plane(7 * cap_x, cap_x, 0)

    deep_node, deep_lane = iota((LANES, LANES), 0), iota((LANES, LANES), 1)
    for dy in (-1, 0, 1):
        part = slice((dy + 1) * LANES, (dy + 2) * LANES)
        start = (bj + 1 + dy) * 16
        gather_map[part, :] = flag(deep_lane == start + deep_node // 8).astype(jnp.bfloat16)
        spread_map[:, part] = flag(deep_node == start + deep_lane // 8).astype(jnp.bfloat16)
    grid_row = iota((8, LANES), 0)
    row32 = iota((ROWS, LANES), 0)
    chunk = 4 * ROWS
    chunks = (7 * cap_x + 4) // 4

    def coarse_sums(ref, assembled):
        def add(i, value):
            return value + jnp.sum(
                ref[pl.ds(pl.multiple_of(i * chunk, chunk), chunk), :].reshape(4, ROWS, LANES), axis=0
            )

        middle = lax.fori_loop(0, chunks, add, zero_plane, unroll=True)
        low, high = 0.5 * has_left * ref[0:ROWS, :], 0.5 * has_right * high_plane(ref)
        sums = [jnp.zeros((8, LANES), jnp.float32)] * 3
        middle = middle - low - high
        for dx, value in ((0, middle),) if assembled else ((-1, low), (0, middle), (1, high)):
            below = 0.5 * has_below * value[0:1, :]
            above = 0.5 * has_above * high_row(value)
            centre = jnp.sum(value, axis=0, keepdims=True) - below - above
            for k, profile in ((1, centre),) if assembled else enumerate((below, centre, above)):
                sums[k] = sums[k] + jnp.where(grid_row == bi + 1 + dx, profile, 0.0)
        return exact_dot(jnp.concatenate(sums, axis=1), gather_map[...])

    def wait_in(buffer, count, send, recv):
        part = buffer.at[pl.ds(0, count)]
        remote(part, part, send, recv, beside(1, 0)).wait_recv()

    def wait_out(buffer, count, send, recv):
        part = buffer.at[pl.ds(0, count)]
        remote(part, part, send, recv, beside(1, 0)).wait_send()

    def exchange_start(source, target, count, me, device, send, recv):
        def go(o, _):
            remote(source, target.at[me], send, recv, device(lax.rem(me + o, count))).start()
            return 0

        lax.fori_loop(1, count, go, 0, unroll=True)
        target[me] = source[...]

    def reduce_start(a, ref, assembled=False):
        grid_s[a] = coarse_sums(ref, assembled)
        exchange_start(
            grid_s.at[a], grid_r.at[a], near, mine, in_block, r_send.at[a, 0], r_recv.at[a, 0]
        )

    lane = iota((1, LANES), 1)

    def scalar_row(values):
        result = jnp.zeros((1, LANES), jnp.float32)
        for i, value in enumerate(values):
            result = jnp.where(lane == i, value, result)
        return result

    def pick(values, i):
        return total(jnp.where(lane == i, values, 0.0))

    grid_rows, grid_lanes = bx + 2, (by + 2) * 16

    def reduce_middle(a, scalars, inner=False):
        wait_in(grid_r.at[a], near - 1, r_send.at[a, 0], r_recv.at[a, 0])
        turned = jnp.sum(grid_r[a], axis=0).T
        value = jnp.zeros((8, width), jnp.float32)
        rim = 1 if inner else 0
        part = slice(16 * rim, grid_lanes - 16 * rim)
        for i in range(rim, grid_rows - rim):
            product = rows_x[i, part, :] * turned[part, i : i + 1]
            value = value + jnp.sum(product.reshape(-1, 8, width), axis=0)
        value = jnp.sum(value, axis=0, keepdims=True)
        for g in range(groups):
            chunk_s[a, g : g + 1, :] = value[:, g * LANES : (g + 1) * LANES]
        chunk_s[a, groups : groups + 1, :] = scalar_row(scalars)
        exchange_start(
            chunk_s.at[a], chunk_r.at[a], far, block_id, across, r_send.at[a, 1], r_recv.at[a, 1]
        )

    def reduce_finish(a, extra, inner=False):
        wait_in(chunk_r.at[a], far - 1, r_send.at[a, 1], r_recv.at[a, 1])
        sums = jnp.sum(chunk_r[a], axis=0)
        through = sums[0:groups, :]
        turned = jnp.zeros((grid_lanes, LANES), jnp.float32)
        wide_lane = iota((grid_lanes, LANES), 1)
        rim = 1 if inner else 0
        for i in range(rim, grid_rows - rim):
            product = rows_x[i, :, 0:LANES] * through[0:1, :]
            for g in range(1, groups):
                product = product + rows_x[i, :, g * LANES : (g + 1) * LANES] * through[g : g + 1, :]
            turned = jnp.where(wide_lane == i, jnp.sum(product, axis=1, keepdims=True), turned)
        turned = jnp.concatenate(
            [turned, jnp.zeros((LANES - grid_lanes, LANES), jnp.float32)], axis=0
        )
        scalars = sums[groups : groups + 1, :]
        if extra is not None:
            scalars = jnp.where(lane == 8, extra, scalars)
        back_s[a] = jnp.where(grid_row == 7, scalars, turned.T[0:8, :])
        exchange_start(
            back_s.at[a], back_r.at[a], near, mine, in_block, r_send.at[a, 2], r_recv.at[a, 2]
        )
        wait_in(back_r.at[a], near - 1, r_send.at[a, 2], r_recv.at[a, 2])
        grid = jnp.sum(back_r[a], axis=0)
        wait_out(grid_r.at[a], near - 1, r_send.at[a, 0], r_recv.at[a, 0])
        wait_out(chunk_r.at[a], far - 1, r_send.at[a, 1], r_recv.at[a, 1])
        wait_out(back_r.at[a], near - 1, r_send.at[a, 2], r_recv.at[a, 2])
        return grid, grid[7:8, :], through

    def coarse_planes(grid):
        deep_values = exact_dot(grid, spread_map[...])

        def spread(dx):
            line = jnp.sum(jnp.where(iota((8, 3 * LANES), 0) == bi + 1 + dx, deep_values, 0.0), axis=0, keepdims=True)
            below, centre, above = (line[:, k * LANES : (k + 1) * LANES] for k in range(3))
            value = jnp.where(row32 == 0, centre + 0.5 * has_below * (below - centre), centre)
            return jnp.where(row32 == end_y, value + 0.5 * has_above * (above - centre), value)

        middle = spread(0)
        first = middle + 0.5 * has_left * (spread(-1) - middle)
        second = middle + 0.5 * has_right * (spread(1) - middle)
        return first, middle, second

    def coarse_at(x, planes):
        first, middle, second = planes
        return jnp.where(x == 0, first, jnp.where(x == end_x, second, middle))

    def apply_operator():
        def along_x(e, carried):
            values = [f_z[plane(7 * e + c), :] for c in range(8)]
            sums = [values[c] + values[7 - c] for c in range(4)]
            gaps = [values[c] - values[7 - c] for c in range(4)]
            scale = e_px[plane(e + 1), :]
            results = [None] * 8
            for b in range(4):
                even = sum(float(0.5 * (STIFF[b, c] + STIFF[b, 7 - c])) * sums[c] for c in range(4))
                odd = sum(float(0.5 * (STIFF[b, c] - STIFF[b, 7 - c])) * gaps[c] for c in range(4))
                results[b] = scale * (even + odd)
                results[7 - b] = scale * (even - odd)
            f_im[plane(7 * e), :] = carried + results[0]
            for b in range(1, 7):
                f_im[plane(7 * e + b), :] = results[b]
            return results[7]

        carried = lax.fori_loop(0, cap_x, along_x, zero_plane, unroll=True)
        f_im[plane(7 * cap_x), :] = carried

        def along_rest(i, product):
            rows = pl.ds(pl.multiple_of(i * chunk, chunk), chunk)
            value = f_z[rows, :]
            high = value.astype(jnp.bfloat16)
            low = (value - high.astype(jnp.float32)).astype(jnp.bfloat16)
            deep = jnp.dot(
                jnp.concatenate([high, low, high], axis=1),
                vertical_ref[...],
                preferred_element_type=jnp.float32,
            )
            wide = jnp.dot(
                across_ref[...],
                jnp.concatenate([high, low, high], axis=0),
                preferred_element_type=jnp.float32,
            )
            image = f_im[rows, :] + f_mass[rows, :] * value
            image = image + f_ya[rows, :] * wide[0:chunk] + f_yb[rows, :] * wide[chunk:]
            image = image + f_za[rows, :] * deep[:, 0:LANES] + f_zb[rows, :] * deep[:, LANES:]
            f_im[rows, :] = image
            return product + jnp.sum((value * image).reshape(chunk // 8, 8, LANES), axis=0)

        product = lax.fori_loop(0, chunks, along_rest, jnp.zeros((8, LANES), jnp.float32), unroll=True)
        return total(product)

    diagonal_copies = halo_start(1, f_inv)
    halo_finish(0, f_r, load_copies)
    reduce_start(0, f_r, True)

    own_rows.wait()

    def scatter_wait(o, _):
        scatter_copy(o).wait()
        return 0

    lax.fori_loop(1, near, scatter_wait, 0)
    spans = {1: (slice(bx, bx + 1), slice(0, 1)), -1: (slice(1, 2), slice(bx + 1, bx + 2))}
    spans[0] = (slice(1, bx + 1), slice(1, bx + 1))
    across_spans = {1: (by, 0, 1), -1: (1, by + 1, 1), 0: (1, 1, by)}
    ring = []
    for k, (dx, dy) in enumerate(DIRECTIONS):
        (source_x, target_x), (source_y, target_y, count) = spans[dx], across_spans[dy]
        copy = remote(
            rows_x.at[source_x, pl.ds(source_y * 16, count * 16), :],
            rows_x.at[target_x, pl.ds(target_y * 16, count * 16), :],
            ring_send.at[k],
            ring_recv.at[k],
            beside(dx * bx, dy * by),
        )
        ring.append(copy)

    halo_finish(1, f_inv, diagonal_copies)
    share_low = jnp.where(row32 == 0, 1.0 - 0.5 * has_below, 1.0)
    share_row = jnp.where(row32 == end_y, 1.0 - 0.5 * has_above, share_low)

    def share_x(x):
        low = jnp.where(x == 0, 1.0 - 0.5 * has_left, 1.0)
        return jnp.where(x == end_x, 1.0 - 0.5 * has_right, low)

    def invert(x, value):
        diagonal = f_inv[plane(x), :]
        inverse = jnp.where(diagonal > 0.0, 1.0 / jnp.where(diagonal > 0.0, diagonal, 1.0), 0.0)
        f_inv[plane(x), :] = inverse
        share = jnp.where(diagonal > 0.0, share_row * share_x(x), 0.0)
        f_share[plane(x), :] = share
        resid = f_r[plane(x), :]
        f_sol[plane(x), :] = zero_plane
        f_w[plane(x), :] = zero_plane
        f_d[plane(x), :] = zero_plane
        return value + share * inverse * resid * resid

    planes = 7 * cap_x + 1
    jacobi = total(lax.fori_loop(0, planes, invert, zero_plane))
    for copy in ring[2:4]:
        copy.start()
    reduce_middle(0, [], True)
    for copy in ring[0:2] + ring[4:]:
        copy.start()
    for copy in ring[2:4]:
        copy.wait()
    grid, _, through = reduce_finish(0, None, True)
    line_s[...] = jnp.sum(jnp.where(grid_row == bi + 1, grid, 0.0), axis=0, keepdims=True)
    lines = [
        remote(line_s, line_r.at[k], line_send.at[k], line_recv.at[k], beside(dx, 0))
        for k, dx in enumerate((1, -1))
    ]
    for copy in lines:
        copy.start()
    for copy in lines:
        copy.wait()
    grid = jnp.where(grid_row == bi, line_r[0], jnp.where(grid_row == bi + 2, line_r[1], grid))
    coarse = coarse_planes(grid)

    def begin(x, _):
        inverse = f_inv[plane(x), :]
        value = jnp.where(inverse > 0.0, coarse_at(x, coarse), 0.0)
        f_z[plane(x), :] = inverse * f_r[plane(x), :] + value
        return 0

    lax.fori_loop(0, planes, begin, 0, unroll=True)

    cross = jnp.zeros((1, 1), jnp.float32)
    beta, rho, curvature = cross, None, cross
    through_w, grid_w = jnp.zeros_like(through), jnp.zeros_like(grid)

    def scalars_of(values, squared):
        rho_now = pick(values, 2) + squared
        beta_now = jnp.zeros((1, 1), jnp.float32) if rho is None else rho_now / rho
        bent = pick(values, 0) + 2.0 * beta_now * pick(values, 1) + beta_now * beta_now * curvature
        return rho_now, beta_now, bent

    for i in range(ITERS):
        own = apply_operator()
        squared = total(through * through)
        if i + 1 < ITERS:
            reduce_start(i + 1, f_im)
            image_copies = halo_start(2 + i, f_im)
            if i == 0:
                for copy in ring[0:2] + ring[4:]:
                    copy.wait()
            reduce_middle(i + 1, [own, cross, jacobi])
            halo_finish(2 + i, f_im, image_copies)
            grid_q, values, through_q = reduce_finish(i + 1, squared)
            rho, beta, curvature = scalars_of(values, pick(values, 8))
            step = rho / curvature
            grid_w = grid_q + beta * grid_w
            through_w = through_q + beta * through_w
            grid = grid - step * grid_w
            through = through - step * through_w
            coarse = coarse_planes(grid)

            def advance(x, sums):
                here = plane(x)
                old = f_z[here, :]
                direction = old + beta * f_d[here, :]
                image = f_im[here, :] + beta * f_w[here, :]
                f_d[here, :] = direction
                f_w[here, :] = image
                f_sol[here, :] = f_sol[here, :] + step * direction
                resid = f_r[here, :] - step * image
                f_r[here, :] = resid
                scaled = f_inv[here, :] * resid
                share = f_share[here, :]
                value = scaled + jnp.where(share > 0.0, coarse_at(x, coarse), 0.0)
                f_z[here, :] = value
                return sums[0] + share * scaled * resid, sums[1] + share * value * image

            jacobi, cross = lax.fori_loop(
                0, planes, advance, (zero_plane, zero_plane), unroll=True
            )
            jacobi, cross = total(jacobi), total(cross)
        else:
            last_s[...] = scalar_row([own, cross, jacobi])
            exchange_start(last_s, last_r, far, block_id, across, l_send.at[0], l_recv.at[0])
            image_copies = halo_start(2 + i, f_im)
            halo_finish(2 + i, f_im, image_copies)
            wait_in(last_r, far - 1, l_send.at[0], l_recv.at[0])
            end_s[...] = jnp.where(lane == 8, squared, jnp.sum(last_r[...], axis=0))
            exchange_start(end_s, end_r, near, mine, in_block, l_send.at[1], l_recv.at[1])
            wait_in(end_r, near - 1, l_send.at[1], l_recv.at[1])
            values = jnp.sum(end_r[...], axis=0)
            rho, beta, curvature = scalars_of(values, pick(values, 8))
            step = rho / curvature
            wait_out(last_r, far - 1, l_send.at[0], l_recv.at[0])
            wait_out(end_r, near - 1, l_send.at[1], l_recv.at[1])

    def put(target, x, value):
        last = high_row(value)
        rows = value[0:slots_y, :]
        rows = jnp.where(row < end_y, rows, jnp.where(row == slots_y - 1, last, 0.0))
        target[x] = rows

    def finish(x, _):
        here = plane(x)
        found = f_sol[here, :] + step * (f_z[here, :] + beta * f_d[here, :])
        resid = f_r[here, :] - step * (f_im[here, :] + beta * f_w[here, :])
        f_sol[here, :] = found
        f_r[here, :] = resid
        put(solution_ref, x, jnp.where(x < end_x, found, 0.0))
        put(residual_ref, x, jnp.where(x < end_x, resid, 0.0))
        return 0

    lax.fori_loop(0, planes, finish, 0, unroll=True)
    put(solution_ref, slots_x - 1, high_plane(f_sol))
    put(residual_ref, slots_x - 1, high_plane(f_r))


def body(nx, ny, right_side, diffusion, kappa, widths_x, widths_y, factor):
    cap_x, cap_y, layers = diffusion.shape
    bx, by = BLOCK, BLOCK
    near, far = bx * by, (nx // bx) * (ny // by)
    groups = factor.shape[1] // (near * LANES)
    f32, bf16 = jnp.float32, jnp.bfloat16
    smem = pl.BlockSpec(memory_space=pltpu.SMEM)
    vmem = pl.BlockSpec(memory_space=pltpu.VMEM)
    hbm = pl.BlockSpec(memory_space=pltpu.HBM)
    tall = cap_x * ROWS
    dma = pltpu.SemaphoreType.DMA
    table = jnp.asarray(tables(cap_x, cap_y, layers))

    def room(*shape, dtype=f32):
        return pltpu.VMEM(shape, dtype)

    scratch = [room(*array.shape) for array in (right_side, diffusion, kappa, table)]
    scratch += [room(3 * LANES, 2 * LANES, dtype=bf16), room(2 * LANES, 3 * LANES, dtype=bf16)]
    scratch += [room(PLANES * ROWS, LANES)] * 13
    scratch += [
        room(tall + 2 * ROWS, LANES),
        room(tall + 2 * ROWS, 3 * LANES),
        room(tall + 2 * ROWS, LANES),
        room(tall + 2 * ROWS, LANES),
        room(LANES, LANES),
        room(LANES, LANES),
        room(bx + 2, (by + 2) * 16, groups * LANES),
        room(3 * LANES, LANES, dtype=bf16),
        room(LANES, 3 * LANES, dtype=bf16),
    ]
    halos = 2 + ITERS
    for _ in range(2):
        scratch += [
            room(halos, 2, ROWS, LANES),
            room(halos, 2, PLANES, LANES),
            room(halos, 4, 8, LANES),
        ]
    scratch += [
        room(ITERS, 8, LANES),
        room(ITERS, near, 8, LANES),
        room(ITERS, groups + 1, LANES),
        room(ITERS, far, groups + 1, LANES),
        room(ITERS, 8, LANES),
        room(ITERS, near, 8, LANES),
        room(1, LANES),
        room(far, 1, LANES),
        room(1, LANES),
        room(near, 1, LANES),
        room(1, LANES),
        room(2, 1, LANES),
        dma((4,)), dma((1,)), dma((near,)), dma((near,)), dma((8,)), dma((8,)),
        dma((halos, 8)), dma((halos, 8)), dma((ITERS, 3)), dma((ITERS, 3)), dma((2,)), dma((2,)),
        dma((2,)), dma((2,)),
    ]
    shape = pltpu.VMEM(right_side.shape, f32)
    return pl.pallas_call(
        functools.partial(kernel, nx, ny, cap_x, cap_y, layers, bx, by),
        out_shape=(shape, shape),
        in_specs=[smem, smem] + [hbm] * 5,
        out_specs=(vmem, vmem),
        scratch_shapes=scratch,
        compiler_params=pltpu.CompilerParams(
            collective_id=0, has_side_effects=True, vmem_limit_bytes=56 * 1024 * 1024
        ),
    )(widths_x, widths_y, right_side, diffusion, kappa, factor, table)


def solution(mesh):
    nx, ny = mesh.shape["gx"], mesh.shape["gy"]
    in_specs = (
        P("gx", "gy", None),
        P("gx", "gy", None),
        P("gx", "gy", None),
        P("gx"),
        P("gy"),
        P(("gx", "gy"), None),
    )
    out_specs = (P("gx", "gy", None), P("gx", "gy", None))
    return jax.shard_map(
        functools.partial(body, nx, ny),
        mesh=mesh,
        in_specs=in_specs,
        out_specs=out_specs,
        check_vma=False,
    )
```
